32 devices in a mesh: dp: 8 (over z, y), row: 2 (over x), col: 2 (over core).
Axes of the slice: x: 2, y: 2, z: 4, core: 2. Of those that a mesh axis runs over, the one named last changes fastest.
Arguments:
- block_input: bfloat16 [73856, 1024], P(('dp', 'col'), 'row'), may hold values from -6 to 6
- image_valid: int32 [128], P('dp'), may hold values 0 or 1
- first_gain: bfloat16 [1024], P('row'), may hold values from 0.5 to 1.5
- first_shift: bfloat16 [1024], P('row'), may hold values from -1.5 to 1.5
- attend_weight: bfloat16 [1024, 3072], P('row', 'col'), may hold values from -0.1875 to 0.1875
- attend_bias: bfloat16 [2048], P('col'), may hold values from -2.5 to 2.5
- output_weight: bfloat16 [1024, 1024], P('col', 'row'), may hold values from -0.75 to 0.75
- output_bias: bfloat16 [1024], P('row'), may hold values from -2.5 to 2.5
- second_gain: bfloat16 [1024], P('row'), may hold values from 0.5 to 1.5
- second_shift: bfloat16 [1024], P('row'), may hold values from -1.5 to 1.5
- expand_weight: bfloat16 [1024, 4096], P('row', 'col'), may hold values from -0.1875 to 0.1875
- expand_bias: bfloat16 [4096], P('col'), may hold values from -2.5 to 2.5
- reduce_weight: bfloat16 [4096, 1024], P('col', 'row'), may hold values from -0.09375 to 0.09375
- reduce_bias: bfloat16 [1024], P('row'), may hold values from -2.5 to 2.5
- output_grad: bfloat16 [73856, 1024], P(('dp', 'col'), 'row'), may hold values from -6 to 6
Outputs:
- block_output: bfloat16 [73856, 1024], P(('dp', 'col'), 'row')
- input_grad: float32 [73856, 1024], P(('dp', 'col'), 'row')
- first_gain_grad: float32 [1024], P('row')
- first_shift_grad: float32 [1024], P('row')
- attend_weight_grad: float32 [1024, 3072], P('row', 'col')
- attend_bias_grad: float32 [2048], P('col')
- output_weight_grad: float32 [1024, 1024], P('col', 'row')
- output_bias_grad: float32 [1024], P('row')
- second_gain_grad: float32 [1024], P('row')
- second_shift_grad: float32 [1024], P('row')
- expand_weight_grad: float32 [1024, 4096], P('row', 'col')
- expand_bias_grad: float32 [4096], P('col')
- reduce_weight_grad: float32 [4096, 1024], P('col', 'row')
- reduce_bias_grad: float32 [1024], P('row')
The draws below stay inside these ranges and needn't reach their ends.
Inputs may be any that keep to these rules, and one draw needn't show every extreme that they name: `image_valid`: 1 marks a real image, 0 a padded slot.
All inputs are finite; a program needn't handle non-finite values. No bound on the sum of `image_valid` on one device may be relied on, other than what follows from the above.
Results may differ from the reference program's by a relative error of at most 0.015.
Values may be sent and summed in bfloat16 or wider, within the bound.
No kernel may reach another device: no remote copies, remote signals or barrier semaphores. Data moves between devices by JAX's collectives and lax.ppermute only.
A program may use at most 576 MiB of HBM per device.

```python
import jax
import jax.numpy as jnp
from jax import lax

D = 1024
HEADS = 16
HD = 64
FF = 4096
SEQ = 577
IMAGES = 128
TOKENS = 73856


def touch_ends(values, rng, least, top_value):
    longest = values.shape.index(max(values.shape))
    spots = []
    for shift in (0, 1):
        where = [jax.random.randint(jax.random.fold_in(rng, axis), (), 0, length) for axis, length in enumerate(values.shape)]
        where[longest] = (where[longest] + shift) % values.shape[longest]
        spots.append(tuple(where))
    return values.at[spots[0]].set(least).at[spots[1]].set(top_value)


def block_scale(key, dims, cuts, least, largest):
    def one(axis_at, shards_of):
        draws = jax.random.uniform(jax.random.fold_in(jax.random.fold_in(key, 6), axis_at), (shards_of,), jnp.float32, least / len(cuts), largest / len(cuts))
        return jnp.repeat(jnp.exp(draws), dims[axis_at] // shards_of).reshape((-1,) + (1,) * (len(dims) - axis_at - 1))

    level = one(*cuts[0])
    for cut in cuts[1:]:
        level = level * one(*cut)
    return level


def normal_values(rng, extent, width, bound, cuts=(), held_as=jnp.bfloat16):
    array = jax.random.normal(rng, extent, jnp.float32) * width
    if len(cuts) > 0:
        array = block_scale(rng, extent, cuts, -0.22, 0.18) * array
    return jnp.clip(array, min=-bound, max=bound).astype(held_as)


def setup_inputs(seed: int = 0) -> dict:
    streams_of = jax.random.split(jax.random.key(seed), 16)
    return {
        "block_input": normal_values(streams_of[0], (TOKENS, D), 1.0, 6.0, ((0, 16), (1, 2))),
        "image_valid": touch_ends((jax.random.randint(streams_of[1], (IMAGES,), 0, 4) < 3).astype(jnp.int32), jax.random.fold_in(streams_of[1], 1), 0, 1),
        "first_gain": jnp.clip(1.0 + 0.1 * jax.random.normal(streams_of[2], (D,), jnp.float32), 0.5, 1.5).astype(jnp.bfloat16),
        "first_shift": normal_values(streams_of[3], (D,), 0.3, 1.5, ((0, 2),)),
        "attend_weight": normal_values(streams_of[4], (D, 3 * D), D ** -0.5, 0.1875, ((0, 2), (1, 2))),
        "attend_bias": normal_values(streams_of[5], (2 * D,), 0.5, 2.5, ((0, 2),)),
        "output_weight": normal_values(streams_of[6], (D, D), HD ** -0.5, 0.75, ((0, 2), (1, 2))),
        "output_bias": normal_values(streams_of[7], (D,), 0.5, 2.5, ((0, 2),)),
        "second_gain": jnp.clip(1.0 + 0.1 * jax.random.normal(streams_of[8], (D,), jnp.float32), 0.5, 1.5).astype(jnp.bfloat16),
        "second_shift": normal_values(streams_of[9], (D,), 0.3, 1.5, ((0, 2),)),
        "expand_weight": normal_values(streams_of[10], (D, FF), D ** -0.5, 0.1875, ((0, 2), (1, 2))),
        "expand_bias": normal_values(streams_of[11], (FF,), 0.5, 2.5, ((0, 2),)),
        "reduce_weight": normal_values(streams_of[12], (FF, D), FF ** -0.5, 0.09375, ((0, 2), (1, 2))),
        "reduce_bias": normal_values(streams_of[13], (D,), 0.5, 2.5, ((0, 2),)),
        "output_grad": normal_values(streams_of[14], (TOKENS, D), 1.0, 6.0, ((0, 16), (1, 2))),
    }


EPSILON = 1e-06
HIGHEST = lax.Precision.HIGHEST

@jax.custom_vjp
def low(v):
    return lax.optimization_barrier(v.astype(jnp.bfloat16)).astype(jnp.float32)

@jax.custom_vjp
def low_back(v):
    return v

def low_keep(v):
    return (low(v), None)

def low_pass(kept, grad):
    return (grad,)

def back_keep(v):
    return (v, None)

def back_low(kept, grad):
    return (low(grad),)
low.defvjp(low_keep, low_pass)
low_back.defvjp(back_keep, back_low)

def matmul(left, right):
    return jnp.dot(left, right, precision=HIGHEST, preferred_element_type=jnp.float32)

def layer_norm(values, gain, shift):
    center = lax.optimization_barrier(jnp.mean(values, -1, keepdims=True))
    spread = lax.optimization_barrier(jnp.mean(values * values, -1, keepdims=True)) - center * center
    return (values - center) * lax.rsqrt(spread + EPSILON) * gain + shift

def attention(packed):
    queries = packed[:, :, :, 0]
    keys_in = packed[:, :, :, 1]
    values_in = packed[:, :, :, 2]
    scores = low_back(jnp.einsum('bqhd,bkhd->bhqk', queries, keys_in, precision=HIGHEST) * HD ** (-0.5))
    weights = jax.nn.softmax(scores, axis=-1)
    mixed = jnp.einsum('bhqk,bkhd->bqhd', low(weights), values_in, precision=HIGHEST)
    return low(low_back(mixed))

def block_forward(params, inputs, valid_rows):
    first_gain, first_shift, attend_weight, attend_bias, output_weight, output_bias, second_gain, second_shift, expand_weight, expand_bias, reduce_weight, reduce_bias = params
    row_count = inputs.shape[0]
    image_count = row_count // SEQ
    first_normed = low(layer_norm(inputs, first_gain, first_shift))
    bias_pairs = attend_bias.reshape(HEADS, 2, HD)
    bias_full = jnp.stack([bias_pairs[:, 0], jnp.zeros_like(bias_pairs[:, 0]), bias_pairs[:, 1]], 1).reshape(3 * D)
    packed = low(low_back(matmul(first_normed, attend_weight) + bias_full))
    mixed = attention(packed.reshape(image_count, SEQ, HEADS, 3, HD)).reshape(row_count, D)
    middle = inputs + low_back(matmul(mixed, output_weight)) + output_bias
    second_normed = low(layer_norm(middle, second_gain, second_shift))
    before = low_back(matmul(second_normed, expand_weight) + expand_bias)
    hidden = low(jax.nn.gelu(before, approximate=False))
    return (middle + low_back(matmul(hidden, reduce_weight)) + reduce_bias) * valid_rows[:, None]

def reference(block_input, image_valid, first_gain, first_shift, attend_weight, attend_bias, output_weight, output_bias, second_gain, second_shift, expand_weight, expand_bias, reduce_weight, reduce_bias, output_grad):
    params = (first_gain.astype(jnp.float32), first_shift.astype(jnp.float32), attend_weight.astype(jnp.float32), attend_bias.astype(jnp.float32), output_weight.astype(jnp.float32), output_bias.astype(jnp.float32), second_gain.astype(jnp.float32), second_shift.astype(jnp.float32), expand_weight.astype(jnp.float32), expand_bias.astype(jnp.float32), reduce_weight.astype(jnp.float32), reduce_bias.astype(jnp.float32))
    step_count = IMAGES // 8
    step_rows = 8 * SEQ
    inputs = block_input.astype(jnp.float32).reshape(step_count, step_rows, D)
    valid_all = jnp.repeat(image_valid.astype(jnp.float32), SEQ).reshape(step_count, step_rows)

    def forward(params_in, inputs_in):
        stepper = jax.checkpoint(block_forward)

        def one_group(pieces):
            return stepper(params_in, pieces[0], pieces[1])
        return lax.map(one_group, (inputs_in, valid_all))
    result, pullback = jax.vjp(forward, params, inputs)
    grads, input_grad = pullback(output_grad.astype(jnp.float32).reshape(step_count, step_rows, D))
    return (result.reshape(TOKENS, D).astype(jnp.bfloat16), input_grad.reshape(TOKENS, D), grads[0], grads[1], grads[2], grads[3], grads[4], grads[5], grads[6], grads[7], grads[8], grads[9], grads[10], grads[11])
```

```python
from functools import partial

import jax
import jax.numpy as jnp
from jax import lax
from jax.experimental import pallas as pl
from jax.experimental.pallas import tpu as pltpu
from jax.sharding import PartitionSpec as P

D = 1024
HD = 64
SEQ = 577
PAD = 592
EPSILON = 1e-06
BF = jnp.bfloat16
F32 = jnp.float32
LOG2E = 1.4426950408889634
ROOT_HALF = 0.7071067811865476
DENSITY = 0.3989422804014327
KEYS_A = 512
MEBI = 1 << 20


def dot_nn(left, right):
    return lax.dot_general(left, right, (((1,), (0,)), ((), ())), preferred_element_type=F32)


def dot_nt(left, right):
    return lax.dot_general(left, right, (((1,), (1,)), ((), ())), preferred_element_type=F32)


def dot_tn(left, right):
    return lax.dot_general(left, right, (((0,), (0,)), ((), ())), preferred_element_type=F32)


def whole(array):
    return pl.BlockSpec(array.shape, lambda *_: (0,) * array.ndim, pipeline_mode=pl.Buffered(1))


def by_image(width):
    return pl.BlockSpec((PAD, width), lambda i: (i, 0))


def call(kernel, name, grid, operands, outputs, macs, after=(), into=None):
    if into is not None:
        after = (into, *after)
    size = sum(a.size * a.dtype.itemsize for _, a in operands)
    size += sum(jnp.dtype(t).itemsize * s[0] * s[1] for _, s, t in outputs)
    used = len(operands)

    def body_of(*refs):
        kernel(*refs[:used], *refs[used + len(after) :])

    return pl.pallas_call(
        body_of,
        grid=grid,
        in_specs=[s for s, _ in operands] + [pl.BlockSpec(memory_space=pl.ANY)] * len(after),
        out_specs=[s for s, _, _ in outputs],
        out_shape=[jax.ShapeDtypeStruct(s, t) for _, s, t in outputs],
        compiler_params=pltpu.CompilerParams(vmem_limit_bytes=60 * MEBI),
        cost_estimate=pl.CostEstimate(flops=4 * macs, bytes_accessed=size, transcendentals=0),
        input_output_aliases={} if into is None else {used: 0},
        name=name,
    )(*[a for _, a in operands], *after)


def shift(values, axis, step):
    size = lax.axis_size(axis)
    return lax.ppermute(values, axis, [(i, (i + step) % size) for i in range(size)])


def gather_blocks(block, axis):
    return [block] + [shift(block, axis, -s) for s in range(1, lax.axis_size(axis))]


def gather_weight(weight):
    return [gather_blocks(block, "col") for block in gather_blocks(weight, "row")]


def fetch_shares(weight):
    depth = weight.shape[0] // lax.axis_size("dp")
    share = lax.dynamic_slice_in_dim(weight, lax.axis_index("dp") * depth, depth)
    return gather_blocks(share, "row")[1:]


def gather_shares(weight, shares):
    blocks = [weight] + [lax.all_gather(s, "dp", axis=0, tiled=True) for s in shares]
    return [gather_blocks(block, "col") for block in blocks]


def hold(values, after):
    return lax.optimization_barrier((values, after))[0]


def swap(values, axis, step):
    return lax.ppermute(values, axis, [(i, i ^ step) for i in range(lax.axis_size(axis))])


def steps_of(axis):
    steps = [1]
    while steps[-1] * 2 < lax.axis_size(axis):
        steps.append(steps[-1] * 2)
    return steps


def sum_all(values, axis):
    for step in steps_of(axis):
        values = values + swap(values, axis, step)
    return values


def halve(values, axis, step):
    half = values.shape[0] // 2
    bit = lax.axis_index(axis) // step % 2
    keep = lax.dynamic_slice_in_dim(values, bit * half, half)
    give = lax.dynamic_slice_in_dim(values, (1 - bit) * half, half)
    return (keep.astype(F32) + swap(give, axis, step).astype(F32)).astype(BF)


def join(values, axis, step):
    other = swap(values, axis, step)
    low = lax.axis_index(axis) // step % 2 == 0
    return jnp.where(low, jnp.concatenate([values, other]), jnp.concatenate([other, values]))


def finish_sum(values, axis):
    steps = steps_of(axis)
    for step in steps[1:]:
        values = halve(values, axis, step)
    for step in reversed(steps):
        values = join(values, axis, step)
    return values


def pack_kernel(place_ref, x_ref, *refs):
    o_refs = refs[-lax.axis_size("row") :]
    images = o_refs[0].shape[0] // PAD
    for place in range(len(o_refs)):

        @pl.when(place_ref[0] == place)
        def _(place=place):
            for s, o_ref in enumerate(o_refs):
                at = (place - s) % len(o_refs) * images
                for i in range(images):
                    rows = x_ref[(at + i) * SEQ : (at + i + 1) * SEQ]
                    o_ref[i * PAD : i * PAD + SEQ] = rows
                    rest = (PAD - SEQ, x_ref.shape[1])
                    o_ref[i * PAD + SEQ : (i + 1) * PAD] = jnp.zeros(rest, x_ref.dtype)


def pack_rows(values, place, after=()):
    rows, width = values.shape
    parts = lax.axis_size("row")
    vmem = pl.BlockSpec(memory_space=pltpu.VMEM)
    part = jax.ShapeDtypeStruct((rows // SEQ // parts * PAD, width), values.dtype)
    return pl.pallas_call(
        pack_kernel,
        in_specs=[pl.BlockSpec(memory_space=pltpu.SMEM), vmem]
        + [pl.BlockSpec(memory_space=pl.ANY)] * len(after),
        out_specs=[vmem] * parts,
        out_shape=[part] * parts,
        compiler_params=pltpu.CompilerParams(vmem_limit_bytes=60 * MEBI),
        cost_estimate=pl.CostEstimate(flops=0, bytes_accessed=8 * values.size, transcendentals=0),
        name="pack_rows",
    )(place.reshape(1), values, *after)


def unpack_kernel(counts, place_ref, *refs):
    o_ref = refs[-1]
    for place in range(len(counts)):

        @pl.when(place_ref[0] == place)
        def _(place=place):
            n = 0
            for s, some in enumerate(counts):
                at = (place - s) % len(counts) * sum(some)
                for count in some:
                    for i in range(count):
                        rows = refs[n][i * PAD : i * PAD + SEQ].astype(o_ref.dtype)
                        o_ref[at * SEQ : (at + 1) * SEQ] = rows
                        at += 1
                    n += 1


def unpack_rows(parts, place, dtype):
    counts = tuple(tuple(a.shape[0] // PAD for a in some) for some in parts)
    arrays = [a for some in parts for a in some]
    vmem = pl.BlockSpec(memory_space=pltpu.VMEM)
    return pl.pallas_call(
        partial(unpack_kernel, counts),
        in_specs=[pl.BlockSpec(memory_space=pltpu.SMEM)] + [vmem] * len(arrays),
        out_specs=vmem,
        out_shape=jax.ShapeDtypeStruct(
            (sum(map(sum, counts)) * SEQ, arrays[0].shape[1]), dtype
        ),
        compiler_params=pltpu.CompilerParams(vmem_limit_bytes=60 * MEBI),
        cost_estimate=pl.CostEstimate(
            flops=0, bytes_accessed=16 * len(parts) * arrays[0].size, transcendentals=0
        ),
        name="unpack_rows",
    )(place.reshape(1), *arrays)


def row_mean(blocks):
    return sum(jnp.sum(b, 1, keepdims=True) for b in blocks) / (len(blocks) * blocks[0].shape[1])


def normalize(blocks):
    center = row_mean(blocks)
    inverse = lax.rsqrt(row_mean([b * b for b in blocks]) - center * center + EPSILON)
    return [(b - center) * inverse for b in blocks], inverse


def norm_back(upstream, scaled, inverse, gains):
    grads = [u * g for u, g in zip(upstream, gains)]
    plain = row_mean(grads)
    cross = row_mean([g * x for g, x in zip(grads, scaled)])
    return [inverse * (g - plain - x * cross) for g, x in zip(grads, scaled)]


def cut(values, width):
    return [values[:, at : at + width] for at in range(0, values.shape[1], width)]


def add_rows(ref, values, at=0):
    ref[:, at : at + values.shape[1]] += jnp.sum(values, 0, keepdims=True)


def grid_of(refs, shape):
    outer, inner = shape
    return [refs[i * inner : (i + 1) * inner] for i in range(outer)]


def project_kernel(shape, gain_ref, shift_ref, bias_ref, *refs):
    rows, cols = shape
    x_refs, weights = refs[:rows], grid_of(refs[rows : rows + rows * cols], shape)
    normed_ref, packed_ref = refs[rows + rows * cols :]
    scaled, _ = normalize([x[...].astype(F32) for x in x_refs])
    width = scaled[0].shape[1]
    gains, shifts = cut(gain_ref[...], width), cut(shift_ref[...], width)
    normed = [(x * g + b).astype(BF) for x, g, b in zip(scaled, gains, shifts)]
    for i, n in enumerate(normed):
        normed_ref[:, i * width : (i + 1) * width] = n
    block = weights[0][0].shape[1]
    for j in range(cols):
        total = sum(dot_nn(n, weights[i][j][...]) for i, n in enumerate(normed))
        where = slice(j * block, (j + 1) * block)
        packed_ref[:, where] = (total + bias_ref[:, where]).astype(BF)


def swap_halves(values):
    return jnp.concatenate([values[:, HD:], values[:, :HD]], 1)


def attend_kernel(p_ref, o_ref):
    first, second, third = p_ref[:, :128], p_ref[:, 128:256], p_ref[:, 256:]
    low = lax.broadcasted_iota(jnp.int32, (1, 128), 1) < HD
    zero, one = jnp.zeros((), BF), jnp.ones((), BF)
    queries = (jnp.where(low, first, zero), jnp.where(low, swap_halves(second), zero))
    keys = (swap_halves(first), third)
    values = (jnp.where(low, second, one), jnp.where(low, one, third))
    scale = HD**-0.5 * LOG2E
    keep = lax.broadcasted_iota(jnp.int32, (1, PAD - KEYS_A), 1) < SEQ - KEYS_A
    chunk = PAD // 2
    for start in range(0, PAD, chunk):
        outs = []
        for h in range(2):
            query = queries[h][start : start + chunk]
            sa = dot_nt(query, keys[h][:KEYS_A])
            sb = jnp.where(keep, dot_nt(query, keys[h][KEYS_A:]), -1e30)
            top = jnp.maximum(jnp.max(sa, 1, keepdims=True), jnp.max(sb, 1, keepdims=True))
            top = top * scale
            pa = jnp.exp2(sa * scale - top).astype(BF)
            pb = jnp.exp2(sb * scale - top).astype(BF)
            outs.append(dot_nn(pa, values[h][:KEYS_A]) + dot_nn(pb, values[h][KEYS_A:]))
        mixed, totals = jnp.where(low, outs[0], outs[1]), jnp.where(low, outs[1], outs[0])
        o_ref[start : start + chunk, :] = (mixed / swap_halves(totals)).astype(BF)


def attend(packed, after):
    tokens, width = packed.shape
    pairs = width // (6 * HD)
    return call(
        attend_kernel,
        "attend",
        (pairs, tokens // PAD),
        [(pl.BlockSpec((PAD, 6 * HD), lambda h, i: (i, h)), packed)],
        [(pl.BlockSpec((PAD, 2 * HD), lambda h, i: (i, h)), (tokens, pairs * 2 * HD), BF)],
        tokens * PAD * pairs * 2 * HD * 13,
        after,
    )[0]


def attend_back_kernel(p_ref, g_ref, o_ref):
    first, second, third = p_ref[:, :128], p_ref[:, 128:256], p_ref[:, 256:]
    grad = g_ref[...]
    low = lax.broadcasted_iota(jnp.int32, (1, 128), 1) < HD
    zero = jnp.zeros((), BF)
    turned = [swap_halves(v) for v in (first, second, third)]
    queries = (jnp.where(low, first, zero), jnp.where(low, turned[1], zero))
    keys, values = (turned[0], third), (second, third)
    grads = (jnp.where(low, grad, zero), jnp.where(low, zero, grad))
    query_right = (turned[0], turned[1])
    key_right = (turned[0], turned[2])
    scale = HD**-0.5
    edge = PAD - 16
    keep = lax.broadcasted_iota(jnp.int32, (PAD - edge, 1), 0) < SEQ - edge
    value_grad, key_grad, query_grad = [0.0, 0.0], [0.0, 0.0], [[], []]
    for start in range(0, PAD, 256):
        some = slice(start, min(PAD, start + 256))
        for h in range(2):
            scores = dot_nt(keys[h], queries[h][some])
            weight_grad = dot_nt(values[h], grads[h][some])
            sa, sb = scores[:edge], jnp.where(keep, scores[edge:], -1e30)
            top = jnp.maximum(jnp.max(sa, 0, keepdims=True), jnp.max(sb, 0, keepdims=True))
            top = top * (scale * LOG2E)
            weights = jnp.concatenate(
                [jnp.exp2(s * (scale * LOG2E) - top) for s in (sa, sb)], 0
            )
            weights = weights * (1.0 / jnp.sum(weights, 0, keepdims=True))
            product = weights * weight_grad
            score_low = (product - weights * jnp.sum(product, 0, keepdims=True)).astype(BF)
            value_grad[h] += dot_nn(weights.astype(BF), grad[some])
            key_grad[h] += dot_nn(score_low, query_right[h][some])
            query_grad[h].append(dot_tn(score_low, key_right[h]))
    query_grad = [jnp.concatenate(q, 0) for q in query_grad]
    o_ref[:, :128] = (jnp.where(low, query_grad[0], key_grad[0]) * scale).astype(BF)
    o_ref[:, 128:256] = jnp.where(low, value_grad[0], query_grad[1] * scale).astype(BF)
    o_ref[:, 256:] = jnp.where(low, key_grad[1] * scale, value_grad[1]).astype(BF)


def attend_back(packed, grad, cols, pair, slot, slots, into, after):
    tokens, width = packed.shape
    block = width // (6 * HD) // cols
    return call(
        attend_back_kernel,
        "attend_back",
        (cols, tokens // PAD),
        [
            (pl.BlockSpec((PAD, 6 * HD), lambda j, i: (i, j * block + pair)), packed),
            (pl.BlockSpec((PAD, 2 * HD), lambda j, i: (i, j * block + pair)), grad),
        ],
        [
            (
                pl.BlockSpec((PAD, 6 * HD), lambda j, i: (i, j * slots + slot)),
                (tokens, cols * slots * 6 * HD),
                BF,
            )
        ],
        tokens * PAD * cols * 2 * HD * 32,
        after,
        into,
    )[0]


def output_kernel(shape, bias_ref, gain_ref, shift_ref, mixed_ref, *refs):
    rows, cols = shape
    x_refs, weights = refs[:rows], grid_of(refs[rows : rows + rows * cols], shape)
    middle_ref, normed_ref = refs[rows + rows * cols :]
    block, width = weights[0][0].shape
    mixed = cut(mixed_ref[...], block)
    middle = []
    for i in range(rows):
        total = sum(dot_nn(m, weights[i][j][...]) for j, m in enumerate(mixed))
        where = slice(i * width, (i + 1) * width)
        middle.append(x_refs[i][...].astype(F32) + total + bias_ref[:, where])
        middle_ref[:, where] = middle[-1]
    scaled, _ = normalize(middle)
    for i, x in enumerate(scaled):
        where = slice(i * width, (i + 1) * width)
        normed_ref[:, where] = (x * gain_ref[:, where] + shift_ref[:, where]).astype(BF)


def expand_kernel(shape, bias_ref, normed_ref, *refs):
    rows, cols = shape
    weights = grid_of(refs[: rows * cols], shape)
    hidden_ref, slope_ref = refs[rows * cols :]
    depth, block = weights[0][0].shape
    normed = cut(normed_ref[...], depth)
    for j in range(cols):
        total = sum(dot_nn(n, weights[i][j][...]) for i, n in enumerate(normed))
        where = slice(j * block, (j + 1) * block)
        before = total + bias_ref[:, where]
        below = 0.5 + 0.5 * lax.erf(before * ROOT_HALF)
        hidden_ref[:, where] = (before * below).astype(BF)
        density = jnp.exp2(before * before * (-0.5 * LOG2E)) * DENSITY
        slope_ref[:, where] = (below + before * density).astype(BF)


def reduce_kernel(shape, valid_ref, bias_ref, hidden_ref, middle_ref, *refs):
    rows, cols = shape
    weights, o_refs = grid_of(refs[: rows * cols], shape), refs[rows * cols :]
    block, width = weights[0][0].shape
    valid = valid_ref[pl.program_id(0)].astype(F32)
    for i in range(rows):
        total = sum(
            dot_nn(hidden_ref[:, j * block : (j + 1) * block], weights[i][j][...])
            for j in range(cols)
        )
        where = slice(i * width, (i + 1) * width)
        o_refs[i][...] = ((middle_ref[:, where] + total + bias_ref[:, where]) * valid).astype(BF)


def reduce_back_kernel(shape, valid_ref, slope_ref, *refs):
    rows, cols = shape
    g_refs, weights = refs[:rows], grid_of(refs[rows : rows + rows * cols], shape)
    out_low_ref, before_ref, reduce_bias_ref, expand_bias_ref = refs[rows + rows * cols :]

    @pl.when(pl.program_id(0) == 0)
    def _():
        reduce_bias_ref[...] = jnp.zeros_like(reduce_bias_ref)
        expand_bias_ref[...] = jnp.zeros_like(expand_bias_ref)

    valid = valid_ref[pl.program_id(0)].astype(F32)
    block, width = weights[0][0].shape
    lows = []
    for i, g in enumerate(g_refs):
        grad = g[...].astype(F32) * valid
        add_rows(reduce_bias_ref, grad, i * width)
        lows.append(grad.astype(BF))
        out_low_ref[:, i * width : (i + 1) * width] = lows[-1]
    for j in range(cols):
        total = sum(dot_nt(low, weights[i][j][...]) for i, low in enumerate(lows))
        where = slice(j * block, (j + 1) * block)
        total = total * slope_ref[:, where].astype(F32)
        add_rows(expand_bias_ref, total, j * block)
        before_ref[:, where] = total.astype(BF)


def expand_back_kernel(shape, gain_ref, before_ref, middle_ref, out_low_ref, *refs):
    rows, cols = shape
    count = rows * cols
    expand, output = grid_of(refs[:count], shape), grid_of(refs[count : 2 * count], shape)
    middle_grad_ref, middle_low_ref, mixed_low_ref, gain_grad, shift_grad, bias_grad = refs[2 * count :]

    @pl.when(pl.program_id(0) == 0)
    def _():
        for ref in (gain_grad, shift_grad, bias_grad):
            ref[...] = jnp.zeros_like(ref)

    width, block = expand[0][0].shape
    upstream = [
        sum(dot_nt(before_ref[:, j * block : (j + 1) * block], expand[i][j][...]) for j in range(cols))
        for i in range(rows)
    ]
    scaled, inverse = normalize(cut(middle_ref[...], width))
    parts = norm_back(upstream, scaled, inverse, cut(gain_ref[...], width))
    lows = []
    for i, part in enumerate(parts):
        where = slice(i * width, (i + 1) * width)
        add_rows(gain_grad, upstream[i] * scaled[i], i * width)
        add_rows(shift_grad, upstream[i], i * width)
        grad = out_low_ref[:, where].astype(F32) + part
        add_rows(bias_grad, grad, i * width)
        middle_grad_ref[:, where] = grad
        lows.append(grad.astype(BF))
        middle_low_ref[:, where] = lows[-1]
    heads = output[0][0].shape[0]
    for j in range(cols):
        total = sum(dot_nt(low, output[i][j][...]) for i, low in enumerate(lows))
        mixed_low_ref[:, j * heads : (j + 1) * heads] = total.astype(BF)


def project_back_kernel(shape, parts, gain_ref, middle_ref, *refs):
    rows, cols = shape
    packed, refs = refs[:parts], refs[parts:]
    x_refs, weights = refs[:rows], grid_of(refs[rows : rows + rows * cols], shape)
    refs = refs[rows + rows * cols :]
    o_refs, (gain_grad, shift_grad), bias_grads = refs[:rows], refs[rows : rows + 2], refs[rows + 2 :]

    @pl.when(pl.program_id(0) == 0)
    def _():
        for ref in refs[rows:]:
            ref[...] = jnp.zeros_like(ref)

    width = weights[0][0].shape[0]
    upstream = [0.0] * rows
    at = 0
    for p in range(parts):
        add_rows(bias_grads[p], packed[p][...].astype(F32))
        some = packed[p].shape[1] // cols
        for j in range(cols):
            grad = packed[p][:, j * some : (j + 1) * some]
            for i in range(rows):
                upstream[i] += dot_nt(grad, weights[i][j][:, at : at + some])
        at += some
    scaled, inverse = normalize([x[...].astype(F32) for x in x_refs])
    grads = norm_back(upstream, scaled, inverse, cut(gain_ref[...], width))
    for i, grad in enumerate(grads):
        add_rows(gain_grad, upstream[i] * scaled[i], i * width)
        add_rows(shift_grad, upstream[i], i * width)
        total = middle_ref[:, i * width : (i + 1) * width] + grad
        o_refs[i][...] = total.astype(o_refs[i].dtype)


def outer_kernel(a_ref, b_ref, o_ref):
    o_ref[...] = dot_tn(a_ref[...], b_ref[...]).astype(o_ref.dtype)


def outer(left, right, left_part, right_part, name, after=()):
    tokens = left.shape[0]
    (li, lw), (ri, rw) = left_part, right_part
    bl, br = min(lw, 1024), 1024 if rw % 1024 == 0 else rw
    return call(
        outer_kernel,
        name,
        (lw // bl, rw // br),
        [
            (pl.BlockSpec((tokens, bl), lambda i, j: (0, li * (lw // bl) + i)), left),
            (pl.BlockSpec((tokens, br), lambda i, j: (0, ri * (rw // br) + j)), right),
        ],
        [(pl.BlockSpec((bl, br), lambda i, j: (i, j)), (lw, rw), BF)],
        tokens * lw * rw,
        after,
    )[0]


def body(
    block_input,
    image_valid,
    first_gain,
    first_shift,
    attend_weight,
    attend_bias,
    output_weight,
    output_bias,
    second_gain,
    second_shift,
    expand_weight,
    expand_bias,
    reduce_weight,
    reduce_bias,
    output_grad,
):
    rows, cols = lax.axis_size("row"), lax.axis_size("col")
    row_index, col_index = lax.axis_index("row"), lax.axis_index("col")
    local_rows, width = block_input.shape
    local_images = local_rows // SEQ
    images = local_images // rows
    tokens = images * PAD
    hidden_width = expand_weight.shape[1] * cols
    shape = (rows, cols)
    step = (images,)

    def to_tokens(values, after=()):
        parts = pack_rows(values, row_index, after)
        return [shift(part, "row", -s) if s else part for s, part in enumerate(parts)]

    def from_tokens(parts, dtype):
        parts = [[shift(a, "row", s) if s else a for a in some] for s, some in enumerate(parts)]
        return unpack_rows(parts, row_index, dtype)

    features = jnp.stack(
        [first_gain, first_shift, output_bias, second_gain, second_shift, reduce_bias]
    )
    features = jnp.concatenate(gather_blocks(features, "row"), 1).astype(F32)
    first_gain, first_shift, output_bias, second_gain, second_shift, reduce_bias = jnp.split(
        features, 6, 0
    )
    biases = jnp.stack(gather_blocks(jnp.concatenate([attend_bias, expand_bias]), "col"))
    biases = biases.astype(F32)
    pairs = biases[:, : attend_bias.shape[0]].reshape(-1, 2, HD)
    attend_bias = jnp.stack([pairs[:, 0], jnp.zeros_like(pairs[:, 0]), pairs[:, 1]], 1)
    attend_bias = attend_bias.reshape(1, 3 * D)
    expand_bias = biases[:, -expand_bias.shape[0] :].reshape(1, -1)
    valid = lax.dynamic_slice_in_dim(
        image_valid, col_index * local_images + row_index * images, images
    )

    inputs = to_tokens(block_input)
    attend_blocks = gather_shares(attend_weight, hold(fetch_shares(attend_weight), inputs[0]))
    expand_shares = fetch_shares(hold(expand_weight, inputs[0]))
    output_blocks = gather_weight(hold(output_weight, inputs))

    def flat(blocks):
        return [(whole(b), b) for some in blocks for b in some]

    def row_blocks(arrays):
        return [(by_image(width), a) for a in arrays]

    def full(array):
        return (whole(array), array)

    def image(array):
        return (by_image(array.shape[1]), array)

    def out(columns, dtype):
        return (by_image(columns), (tokens, columns), dtype)

    def total(columns):
        return (pl.BlockSpec((1, columns), lambda i: (0, 0)), (1, columns), F32)

    scalars = (pl.BlockSpec(memory_space=pltpu.SMEM), valid)

    first_normed, packed = call(
        partial(project_kernel, shape),
        "project",
        step,
        [full(first_gain), full(first_shift), full(attend_bias)]
        + row_blocks(inputs)
        + flat(attend_blocks),
        [out(D, BF), out(3 * D, BF)],
        tokens * 3 * D * D,
    )
    grads = to_tokens(output_grad, (packed,))
    expand_blocks = gather_shares(expand_weight, expand_shares)
    reduce_shares = fetch_shares(hold(reduce_weight, packed))
    mixed = attend(packed, (*expand_shares, *reduce_shares, *output_blocks[-1], grads[0]))
    reduce_blocks = gather_shares(reduce_weight, hold(reduce_shares, mixed))
    middle, second_normed = call(
        partial(output_kernel, shape),
        "output",
        step,
        [full(output_bias), full(second_gain), full(second_shift), image(mixed)]
        + row_blocks(inputs)
        + flat(output_blocks),
        [out(D, F32), out(D, BF)],
        tokens * D * D,
    )
    hidden, slope = call(
        partial(expand_kernel, shape),
        "expand",
        step,
        [full(expand_bias), image(second_normed)] + flat(expand_blocks),
        [out(hidden_width, BF), out(hidden_width, BF)],
        tokens * D * hidden_width,
    )
    out_low, before_low, reduce_bias_grad, expand_bias_grad = call(
        partial(reduce_back_kernel, shape),
        "reduce_back",
        step,
        [scalars, image(slope)] + row_blocks(grads) + flat(reduce_blocks),
        [out(D, BF), out(hidden_width, BF), total(D), total(hidden_width)],
        tokens * D * hidden_width,
    )

    def add_parts(parts, axis, after=None):
        held = parts[0].astype(F32)
        others = [shift(part, axis, s) for s, part in enumerate(parts) if s]
        for other in others if after is None else hold(others, after):
            held = held + other.astype(F32)
        return held

    def outer_parts(left, right, over_left, name, after=()):
        lw, rw = left.shape[1], right.shape[1]
        parts = []
        for j in reversed(range(cols)):
            places = ((j, lw // cols), (0, rw)) if over_left else ((0, lw), (j, rw // cols))
            parts.insert(0, outer(left, right, *places, name, parts[:1] or after))
        return parts

    def share_of(held, dim, after=None):
        return add_parts(jnp.split(held, rows, dim), "row", after).astype(BF)

    reduce_held = add_parts(outer_parts(hidden, out_low, True, "reduce_outer"), "col").astype(BF)
    reduce_share = share_of(reduce_held, 1)
    middle_grad, middle_low, mixed_low, second_gain_grad, second_shift_grad, output_bias_grad = call(
        partial(expand_back_kernel, shape),
        "expand_back",
        step,
        [full(second_gain), image(before_low), image(middle), image(out_low)]
        + flat(expand_blocks)
        + flat(output_blocks),
        [out(D, F32), out(D, BF), out(D, BF), total(D), total(D), total(D)],
        tokens * D * (hidden_width + D),
        (reduce_held,),
    )
    expand_held = outer_parts(second_normed, before_low, False, "expand_outer")
    expand_held = add_parts(expand_held, "col").astype(BF)
    output_held = outer_parts(mixed, middle_low, True, "output_outer", (reduce_share,))
    output_held = add_parts(output_held, "col").astype(BF)
    results = call(
        partial(reduce_kernel, shape),
        "reduce",
        step,
        [scalars, full(reduce_bias), image(hidden), image(middle)] + flat(reduce_blocks),
        [out(width, BF)] * rows,
        tokens * D * hidden_width,
        (expand_held, output_held),
    )
    block_output = from_tokens([[r] for r in results], BF)

    expand_share = share_of(expand_held, 0, results[0])
    output_share = share_of(output_held, 1, results[0])
    reduce_weight_grad = lax.psum(reduce_share, "dp")
    expand_weight_grad, output_weight_grad = lax.psum(
        hold((expand_share, output_share), reduce_weight_grad), "dp"
    )
    pairs = 3 * D // (6 * HD) // cols
    counts = [pairs - 2, 1, 1] if pairs > 2 else [pairs]
    packed_lows, held, shares, halved, pair = [], [], [], [], 0
    ready = results[:1]
    for g, count in enumerate(counts):
        packed_low = None
        for slot in range(count):
            packed_low = attend_back(
                packed, mixed_low, cols, pair, slot, count, packed_low, ready
            )
            ready = (expand_share, output_share, reduce_weight_grad) if pair == 0 else ()
            pair += 1
        packed_lows.append(packed_low)
        parts = outer_parts(first_normed, packed_low, False, "project_outer")
        held.append(add_parts(parts, "col").astype(BF))
        shares.append(share_of(held[-1], 0))
        halved.append(halve(shares[-1], "dp", 1))
        ready = (held[g],)
        ready += (shares[g - 1], expand_weight_grad) if g > 0 else ()
    late = jnp.concatenate(halved[:-1], 1) if len(counts) > 1 else halved[0]
    late = finish_sum(hold(late, held[-1]), "dp")
    attend_weight_grad = [late, finish_sum(halved[-1], "dp")] if len(counts) > 1 else [late]
    attend_weight_grad = jnp.concatenate(attend_weight_grad, 1)

    halves = 2 if images % 2 == 0 else 1
    some = images // halves
    input_grads, sums = [], 0.0
    for half in range(halves):

        def later(array):
            place = half * some
            spec = pl.BlockSpec((PAD, array.shape[1]), lambda i: (i + place, 0))
            return (spec, array)

        def here(dtype):
            return (by_image(width), (some * PAD, width), dtype)

        results = call(
            partial(project_back_kernel, shape, len(counts)),
            "project_back",
            (some,),
            [full(first_gain), later(middle_grad)]
            + [later(p) for p in packed_lows]
            + [later(x) for x in inputs]
            + flat(attend_blocks),
            [here(F32)]
            + [here(BF)] * (rows - 1)
            + [total(D), total(D)]
            + [total(p.shape[1]) for p in packed_lows],
            some * PAD * 3 * D * D,
            ready,
        )
        input_grads.append(results[:rows])
        ready = (results[0], shares[-1])
        packed_sums = [v.reshape(cols, -1, 3, HD) for v in results[rows + 2 :]]
        late = (*results[rows : rows + 2], jnp.concatenate(packed_sums, 1))
        sums = late if half == 0 else jax.tree.map(jnp.add, sums, late)
    input_grad = from_tokens(list(zip(*input_grads)), F32)
    first_gain_grad, first_shift_grad, packed_sums = sums

    feature_grads = jnp.concatenate(
        [
            first_gain_grad,
            first_shift_grad,
            output_bias_grad,
            second_gain_grad,
            second_shift_grad,
            reduce_bias_grad,
        ]
    )
    attend_bias_grad = jnp.stack([packed_sums[:, :, 0], packed_sums[:, :, 2]], 2)
    attend_bias_grad = attend_bias_grad.reshape(cols, -1)
    bias_grads = jnp.concatenate([attend_bias_grad, expand_bias_grad.reshape(cols, -1)], 1)
    bias_grads = add_parts(list(bias_grads), "col")
    feature_grads = sum_all(feature_grads.reshape(-1), "col")
    small = sum_all(jnp.concatenate([feature_grads, bias_grads]), "dp")
    feature_grads, bias_grads = small[: 6 * D].reshape(6, D), small[6 * D :]
    feature_grads = add_parts(jnp.split(feature_grads, rows, 1), "row")
    bias_grads = sum_all(bias_grads, "row")
    split = attend_bias_grad.shape[1]
    return (
        block_output,
        input_grad,
        feature_grads[0],
        feature_grads[1],
        attend_weight_grad.astype(F32),
        bias_grads[:split],
        output_weight_grad.astype(F32),
        feature_grads[2],
        feature_grads[3],
        feature_grads[4],
        expand_weight_grad.astype(F32),
        bias_grads[split:],
        reduce_weight_grad.astype(F32),
        feature_grads[5],
    )


def solution(mesh):
    tokens = P(("dp", "col"), "row")
    by_row, by_col = P("row"), P("col")
    up, down = P("row", "col"), P("col", "row")
    params = (by_row, by_row, up, by_col, down, by_row, by_row, by_row, up, by_col, down, by_row)
    return jax.shard_map(
        body,
        mesh=mesh,
        in_specs=(tokens, P("dp")) + params + (tokens,),
        out_specs=(tokens, tokens) + params,
        check_vma=False,
    )
```

```python
from functools import partial

import jax
import jax.numpy as jnp
from jax import lax
from jax.experimental import pallas as pl
from jax.experimental.pallas import tpu as pltpu
from jax.sharding import PartitionSpec as P

D = 1024
HD = 64
SEQ = 577
PAD = 592
EPSILON = 1e-06
BF = jnp.bfloat16
F32 = jnp.float32
LOG2E = 1.4426950408889634
ROOT_HALF = 0.7071067811865476
DENSITY = 0.3989422804014327
KEYS_A = 512
EXPAND_CUT = 1024
LIGHT = 128
QUERY_CUTS = (0, 208, 400, PAD)
MEBI = 1 << 20


def dot_nn(left, right):
    return lax.dot_general(left, right, (((1,), (0,)), ((), ())), preferred_element_type=F32)


def dot_nt(left, right):
    return lax.dot_general(left, right, (((1,), (1,)), ((), ())), preferred_element_type=F32)


def dot_tn(left, right):
    return lax.dot_general(left, right, (((0,), (0,)), ((), ())), preferred_element_type=F32)


def whole(array):
    return pl.BlockSpec(array.shape, lambda *_: (0,) * array.ndim, pipeline_mode=pl.Buffered(1))


def by_image(width):
    return pl.BlockSpec((PAD, width), lambda i: (i, 0))


def call(kernel, name, grid, operands, outputs, macs, after=(), into=None, weight=1):
    if into is not None:
        after = (into, *after)
    size = sum(a.size * a.dtype.itemsize for _, a in operands)
    size += sum(jnp.dtype(t).itemsize * s[0] * s[1] for _, s, t in outputs)
    used = len(operands)

    def body_of(*refs):
        kernel(*refs[:used], *refs[used + len(after) :])

    return pl.pallas_call(
        body_of,
        grid=grid,
        in_specs=[s for s, _ in operands] + [pl.BlockSpec(memory_space=pl.ANY)] * len(after),
        out_specs=[s for s, _, _ in outputs],
        out_shape=[jax.ShapeDtypeStruct(s, t) for _, s, t in outputs],
        compiler_params=pltpu.CompilerParams(vmem_limit_bytes=60 * MEBI),
        cost_estimate=pl.CostEstimate(flops=2 * macs // weight, bytes_accessed=size // weight, transcendentals=0),
        input_output_aliases={} if into is None else {used: 0},
        name=name,
    )(*[a for _, a in operands], *after)


def shift(values, axis, step):
    size = lax.axis_size(axis)
    return lax.ppermute(values, axis, [(i, (i + step) % size) for i in range(size)])


def gather_blocks(block, axis):
    return [block] + [shift(block, axis, -s) for s in range(1, lax.axis_size(axis))]


def gather_weight(weight):
    return [gather_blocks(block, "col") for block in gather_blocks(weight, "row")]


def fetch_shares(weights):
    place = lax.axis_index("dp")
    depths = [w.shape[0] // lax.axis_size("dp") for w in weights]
    shares = [lax.dynamic_slice_in_dim(w, place * d, d) for w, d in zip(weights, depths)]
    widths = [w.shape[1] for w in weights]
    fetched = gather_blocks(jnp.concatenate(shares, 1), "row")[1:]
    ends = [sum(widths[: n + 1]) for n in range(len(widths))]
    return [[f[:, end - w : end] for f in fetched] for end, w in zip(ends, widths)]


def gather_shares(weight, shares, after=None):
    blocks = [lax.all_gather(s, "dp", axis=0, tiled=True) for s in shares]
    blocks = [weight] + (blocks if after is None else hold(blocks, after))
    return [gather_blocks(block, "col") for block in blocks]


def hold(values, after):
    return lax.optimization_barrier((values, after))[0]


def swap(values, axis, step):
    return lax.ppermute(values, axis, [(i, i ^ step) for i in range(lax.axis_size(axis))])


def steps_of(axis):
    steps = [1]
    while steps[-1] * 2 < lax.axis_size(axis):
        steps.append(steps[-1] * 2)
    return steps


def sum_all(values, axis):
    for step in steps_of(axis):
        values = values + swap(values, axis, step)
    return values


def halve(values, axis, step):
    half = values.shape[0] // 2
    bit = lax.axis_index(axis) // step % 2
    keep = lax.dynamic_slice_in_dim(values, bit * half, half)
    give = lax.dynamic_slice_in_dim(values, (1 - bit) * half, half)
    return (keep.astype(F32) + swap(give, axis, step).astype(F32)).astype(BF)


def join(values, axis, step):
    other = swap(values, axis, step)
    low = lax.axis_index(axis) // step % 2 == 0
    return jnp.where(low, jnp.concatenate([values, other]), jnp.concatenate([other, values]))


def sum_shares(values, axis):
    for step in steps_of(axis):
        values = halve(values, axis, step)
    for step in reversed(steps_of(axis)):
        values = join(values, axis, step)
    return values


def pack_kernel(masked, place_ref, valid_ref, x_ref, *refs):
    o_refs = refs[-lax.axis_size("row") :]
    images = o_refs[0].shape[0] // PAD
    for place in range(len(o_refs)):

        @pl.when(place_ref[0] == place)
        def _(place=place):
            for s, o_ref in enumerate(o_refs):
                at = (place - s) % len(o_refs) * images
                for i in range(images):
                    rows = x_ref[(at + i) * SEQ : (at + i + 1) * SEQ]
                    if masked:
                        rows = (rows.astype(F32) * valid_ref[at + i].astype(F32)).astype(rows.dtype)
                    o_ref[i * PAD : i * PAD + SEQ] = rows
                    rest = (PAD - SEQ, x_ref.shape[1])
                    o_ref[i * PAD + SEQ : (i + 1) * PAD] = jnp.zeros(rest, x_ref.dtype)


def pack_rows(values, place, valid, masked, after=()):
    rows, width = values.shape
    parts = lax.axis_size("row")
    vmem, smem = pl.BlockSpec(memory_space=pltpu.VMEM), pl.BlockSpec(memory_space=pltpu.SMEM)
    part = jax.ShapeDtypeStruct((rows // SEQ // parts * PAD, width), values.dtype)
    return pl.pallas_call(
        partial(pack_kernel, masked),
        in_specs=[smem, smem, vmem] + [pl.BlockSpec(memory_space=pl.ANY)] * len(after),
        out_specs=[vmem] * parts,
        out_shape=[part] * parts,
        compiler_params=pltpu.CompilerParams(vmem_limit_bytes=60 * MEBI),
        cost_estimate=pl.CostEstimate(flops=0, bytes_accessed=values.size // 8, transcendentals=0),
        name="pack_rows",
    )(place.reshape(1), valid, values, *after)


def unpack_kernel(counts, place_ref, *refs):
    o_ref = refs[-1]
    for place in range(len(counts)):

        @pl.when(place_ref[0] == place)
        def _(place=place):
            n = 0
            for s, some in enumerate(counts):
                at = (place - s) % len(counts) * sum(some)
                for count in some:
                    for i in range(count):
                        rows = refs[n][i * PAD : i * PAD + SEQ].astype(o_ref.dtype)
                        o_ref[at * SEQ : (at + 1) * SEQ] = rows
                        at += 1
                    n += 1


def unpack_rows(parts, place, dtype):
    counts = tuple(tuple(a.shape[0] // PAD for a in some) for some in parts)
    arrays = [a for some in parts for a in some]
    vmem = pl.BlockSpec(memory_space=pltpu.VMEM)
    return pl.pallas_call(
        partial(unpack_kernel, counts),
        in_specs=[pl.BlockSpec(memory_space=pltpu.SMEM)] + [vmem] * len(arrays),
        out_specs=vmem,
        out_shape=jax.ShapeDtypeStruct(
            (sum(map(sum, counts)) * SEQ, arrays[0].shape[1]), dtype
        ),
        compiler_params=pltpu.CompilerParams(vmem_limit_bytes=60 * MEBI),
        cost_estimate=pl.CostEstimate(
            flops=0, bytes_accessed=arrays[0].size // 8, transcendentals=0
        ),
        name="unpack_rows",
    )(place.reshape(1), *arrays)


def row_mean(blocks):
    return sum(jnp.sum(b, 1, keepdims=True) for b in blocks) / (len(blocks) * blocks[0].shape[1])


def normalize(blocks):
    center = row_mean(blocks)
    inverse = lax.rsqrt(row_mean([b * b for b in blocks]) - center * center + EPSILON)
    return [(b - center) * inverse for b in blocks], inverse


def norm_back(upstream, scaled, inverse, gains):
    grads = [u * g for u, g in zip(upstream, gains)]
    plain = row_mean(grads)
    cross = row_mean([g * x for g, x in zip(grads, scaled)])
    return [inverse * (g - plain - x * cross) for g, x in zip(grads, scaled)]


def cut(values, width):
    return [values[:, at : at + width] for at in range(0, values.shape[1], width)]


def add_rows(ref, values, at=0):
    ref[:, at : at + values.shape[1]] += jnp.sum(values, 0, keepdims=True)


def grid_of(refs, shape):
    outer, inner = shape
    return [refs[i * inner : (i + 1) * inner] for i in range(outer)]


def project_kernel(shape, gain_ref, shift_ref, bias_ref, *refs):
    rows, cols = shape
    x_refs, weights = refs[:rows], grid_of(refs[rows : rows + rows * cols], shape)
    normed_ref, packed_ref = refs[rows + rows * cols :]
    scaled, _ = normalize([x[...].astype(F32) for x in x_refs])
    width = scaled[0].shape[1]
    gains, shifts = cut(gain_ref[...], width), cut(shift_ref[...], width)
    normed = [(x * g + b).astype(BF) for x, g, b in zip(scaled, gains, shifts)]
    for i, n in enumerate(normed):
        normed_ref[:, i * width : (i + 1) * width] = n
    block = weights[0][0].shape[1]
    for j in range(cols):
        total = sum(dot_nn(n, weights[i][j][...]) for i, n in enumerate(normed))
        where = slice(j * block, (j + 1) * block)
        packed_ref[:, where] = (total + bias_ref[:, where]).astype(BF)


def swap_halves(values):
    return jnp.concatenate([values[:, HD:], values[:, :HD]], 1)


def attend_kernel(p_ref, o_ref):
    first, second, third = p_ref[:, :128], p_ref[:, 128:256], p_ref[:, 256:]
    low = lax.broadcasted_iota(jnp.int32, (1, 128), 1) < HD
    zero, one = jnp.zeros((), BF), jnp.ones((), BF)
    queries = (jnp.where(low, first, zero), jnp.where(low, swap_halves(second), zero))
    keys = (swap_halves(first), third)
    values = (jnp.where(low, second, one), jnp.where(low, one, third))
    scale = HD**-0.5 * LOG2E
    keep = lax.broadcasted_iota(jnp.int32, (1, PAD - KEYS_A), 1) < SEQ - KEYS_A
    units = [(slice(*cut), h) for cut in zip(QUERY_CUTS, QUERY_CUTS[1:]) for h in range(2)]
    scores = [
        (dot_nt(queries[h][some], keys[h][:KEYS_A]), dot_nt(queries[h][some], keys[h][KEYS_A:]))
        for some, h in units
    ]
    weights = []
    for sa, sb in scores:
        sb = jnp.where(keep, sb, -1e30)
        top = jnp.maximum(jnp.max(sa, 1, keepdims=True), jnp.max(sb, 1, keepdims=True)) * scale
        weights.append([jnp.exp2(v * scale - top).astype(BF) for v in (sa, sb)])
    outs = [
        dot_nn(pa, values[h][:KEYS_A]) + dot_nn(pb, values[h][KEYS_A:])
        for (_, h), (pa, pb) in zip(units, weights)
    ]
    for n in range(0, len(units), 2):
        mixed, totals = jnp.where(low, *outs[n : n + 2]), jnp.where(low, *outs[n : n + 2][::-1])
        o_ref[units[n][0], :] = (mixed / swap_halves(totals)).astype(BF)


def attend(packed, half, into, after):
    tokens, width = packed.shape
    pairs = width // (6 * HD)
    some = pairs // 2
    return call(
        attend_kernel,
        "attend",
        (some, tokens // PAD),
        [(pl.BlockSpec((PAD, 6 * HD), lambda h, i: (i, half * some + h)), packed)],
        [
            (
                pl.BlockSpec((PAD, 2 * HD), lambda h, i: (i, half * some + h)),
                (tokens, pairs * 2 * HD),
                BF,
            )
        ],
        tokens * PAD * some * 2 * HD * 5,
        after,
        into,
    )[0]


def attend_back_kernel(p_ref, g_ref, o_ref):
    first, second, third = p_ref[:, :128], p_ref[:, 128:256], p_ref[:, 256:]
    grad = g_ref[...]
    low = lax.broadcasted_iota(jnp.int32, (1, 128), 1) < HD
    zero = jnp.zeros((), BF)
    turned = [swap_halves(v) for v in (first, second, third)]
    queries = (jnp.where(low, first, zero), jnp.where(low, turned[1], zero))
    keys, values = (turned[0], third), (second, third)
    grads = (jnp.where(low, grad, zero), jnp.where(low, zero, grad))
    query_right = (turned[0], turned[1])
    key_right = (turned[0], turned[2])
    scale = HD**-0.5
    edge = PAD - 16
    keep = lax.broadcasted_iota(jnp.int32, (PAD - edge, 1), 0) < SEQ - edge
    units = [(slice(at, min(PAD, at + 256)), h) for at in range(0, PAD, 256) for h in range(2)]
    products = [
        (dot_nt(keys[h], queries[h][some]), dot_nt(values[h], grads[h][some])) for some, h in units
    ]
    lows = []
    for scores, weight_grad in products:
        sa, sb = scores[:edge], jnp.where(keep, scores[edge:], -1e30)
        top = jnp.maximum(jnp.max(sa, 0, keepdims=True), jnp.max(sb, 0, keepdims=True))
        top = top * (scale * LOG2E)
        weights = jnp.concatenate([jnp.exp2(s * (scale * LOG2E) - top) for s in (sa, sb)], 0)
        share = 1.0 / jnp.sum(weights, 0, keepdims=True)
        product = weights * weight_grad
        row_dot = jnp.sum(product, 0, keepdims=True) * share
        score_low = (product - weights * row_dot) * share
        lows.append(((weights * share).astype(BF), score_low.astype(BF)))
    value_grad, key_grad, query_grad = [0.0, 0.0], [0.0, 0.0], [[], []]
    for (some, h), (weights, score_low) in zip(units, lows):
        value_grad[h] += dot_nn(weights, grad[some])
        key_grad[h] += dot_nn(score_low, query_right[h][some])
        query_grad[h].append(dot_tn(key_right[h], score_low).T)
    query_grad = [jnp.concatenate(q, 0) for q in query_grad]
    o_ref[:, :128] = (jnp.where(low, query_grad[0], key_grad[0]) * scale).astype(BF)
    o_ref[:, 128:256] = jnp.where(low, value_grad[0], query_grad[1] * scale).astype(BF)
    o_ref[:, 256:] = jnp.where(low, key_grad[1] * scale, value_grad[1]).astype(BF)


def attend_back(packed, grad, cols, pair, slot, slots, into, after):
    tokens, width = packed.shape
    block = width // (6 * HD) // cols
    return call(
        attend_back_kernel,
        "attend_back",
        (cols, tokens // PAD),
        [
            (pl.BlockSpec((PAD, 6 * HD), lambda j, i: (i, j * block + pair)), packed),
            (pl.BlockSpec((PAD, 2 * HD), lambda j, i: (i, j * block + pair)), grad),
        ],
        [
            (
                pl.BlockSpec((PAD, 6 * HD), lambda j, i: (i, j * slots + slot)),
                (tokens, cols * slots * 6 * HD),
                BF,
            )
        ],
        tokens * PAD * cols * 2 * HD * 12,
        after,
        into,
        LIGHT,
    )[0]


def output_kernel(shape, bias_ref, gain_ref, shift_ref, mixed_ref, *refs):
    rows, cols = shape
    x_refs, weights = refs[:rows], grid_of(refs[rows : rows + rows * cols], shape)
    middle_ref, normed_ref = refs[rows + rows * cols :]
    block, width = weights[0][0].shape
    mixed = cut(mixed_ref[...], block)
    middle = []
    for i in range(rows):
        total = sum(dot_nn(m, weights[i][j][...]) for j, m in enumerate(mixed))
        where = slice(i * width, (i + 1) * width)
        middle.append(x_refs[i][...].astype(F32) + total + bias_ref[:, where])
        middle_ref[:, where] = middle[-1]
    scaled, _ = normalize(middle)
    for i, x in enumerate(scaled):
        where = slice(i * width, (i + 1) * width)
        normed_ref[:, where] = (x * gain_ref[:, where] + shift_ref[:, where]).astype(BF)


def expand_kernel(shape, bias_ref, normed_ref, *refs):
    rows, cols = shape
    weights = grid_of(refs[: rows * cols], shape)
    hidden_ref, slope_ref = refs[rows * cols :]
    depth, block = weights[0][0].shape
    normed = cut(normed_ref[...], depth)
    some = min(block, EXPAND_CUT)
    cuts = [(j, at) for j in range(cols) for at in range(0, block, some)]
    totals = [
        sum(dot_nn(n, weights[i][j][:, at : at + some]) for i, n in enumerate(normed))
        for j, at in cuts
    ]
    for (j, at), total in zip(cuts, totals):
        where = slice(j * block + at, j * block + at + some)
        before = total + bias_ref[:, where]
        below = 0.5 + 0.5 * lax.erf(before * ROOT_HALF)
        hidden_ref[:, where] = (before * below).astype(BF)
        density = jnp.exp2(before * before * (-0.5 * LOG2E)) * DENSITY
        slope_ref[:, where] = (below + before * density).astype(BF)


def reduce_kernel(shape, valid_ref, bias_ref, hidden_ref, middle_ref, *refs):
    rows, cols = shape
    weights, o_refs = grid_of(refs[: rows * cols], shape), refs[rows * cols :]
    block, width = weights[0][0].shape
    valid = valid_ref[pl.program_id(0)].astype(F32)
    for i in range(rows):
        total = sum(
            dot_nn(hidden_ref[:, j * block : (j + 1) * block], weights[i][j][...])
            for j in range(cols)
        )
        where = slice(i * width, (i + 1) * width)
        o_refs[i][...] = ((middle_ref[:, where] + total + bias_ref[:, where]) * valid).astype(BF)


def reduce_back_kernel(shape, slope_ref, *refs):
    rows, cols = shape
    g_refs, weights = refs[:rows], grid_of(refs[rows : rows + rows * cols], shape)
    before_ref, reduce_bias_ref, expand_bias_ref = refs[rows + rows * cols :]

    @pl.when(pl.program_id(0) == 0)
    def _():
        reduce_bias_ref[...] = jnp.zeros_like(reduce_bias_ref)
        expand_bias_ref[...] = jnp.zeros_like(expand_bias_ref)

    block, width = weights[0][0].shape
    lows = [g[...] for g in g_refs]
    for i, low in enumerate(lows):
        add_rows(reduce_bias_ref, low.astype(F32), i * width)
    for j in range(cols):
        total = sum(dot_nt(low, weights[i][j][...]) for i, low in enumerate(lows))
        where = slice(j * block, (j + 1) * block)
        total = total * slope_ref[:, where].astype(F32)
        add_rows(expand_bias_ref, total, j * block)
        before_ref[:, where] = total.astype(BF)


def expand_back_kernel(shape, gain_ref, before_ref, middle_ref, *refs):
    rows, cols = shape
    g_refs, refs = refs[:rows], refs[rows:]
    count = rows * cols
    expand, output = grid_of(refs[:count], shape), grid_of(refs[count : 2 * count], shape)
    refs = refs[2 * count :]
    middle_grad_ref, mixed_low_ref, gain_grad, shift_grad, bias_grad = refs[:5]
    low_refs = refs[5:]

    @pl.when(pl.program_id(0) == 0)
    def _():
        for ref in (gain_grad, shift_grad, bias_grad):
            ref[...] = jnp.zeros_like(ref)

    width, block = expand[0][0].shape
    upstream = [
        sum(dot_nt(before_ref[:, j * block : (j + 1) * block], expand[i][j][...]) for j in range(cols))
        for i in range(rows)
    ]
    scaled, inverse = normalize(cut(middle_ref[...], width))
    parts = norm_back(upstream, scaled, inverse, cut(gain_ref[...], width))
    lows = []
    for i, part in enumerate(parts):
        where = slice(i * width, (i + 1) * width)
        add_rows(gain_grad, upstream[i] * scaled[i], i * width)
        add_rows(shift_grad, upstream[i], i * width)
        grad = g_refs[i][...].astype(F32) + part
        add_rows(bias_grad, grad, i * width)
        middle_grad_ref[:, where] = grad
        lows.append(grad.astype(BF))
        low_refs[i][...] = lows[-1]
    heads = output[0][0].shape[0]
    for j in range(cols):
        total = sum(dot_nt(low, output[i][j][...]) for i, low in enumerate(lows))
        mixed_low_ref[:, j * heads : (j + 1) * heads] = total.astype(BF)


def project_back_kernel(shape, parts, gain_ref, middle_ref, *refs):
    rows, cols = shape
    packed, refs = refs[:parts], refs[parts:]
    x_refs, weights = refs[:rows], grid_of(refs[rows : rows + rows * cols], shape)
    refs = refs[rows + rows * cols :]
    o_refs, (gain_grad, shift_grad), bias_grads = refs[:rows], refs[rows : rows + 2], refs[rows + 2 :]

    @pl.when(pl.program_id(0) == 0)
    def _():
        for ref in refs[rows:]:
            ref[...] = jnp.zeros_like(ref)

    width = weights[0][0].shape[0]
    upstream = [0.0] * rows
    at = 0
    for p in range(parts):
        add_rows(bias_grads[p], packed[p][...].astype(F32))
        some = packed[p].shape[1] // cols
        for j in range(cols):
            grad = packed[p][:, j * some : (j + 1) * some]
            for i in range(rows):
                upstream[i] += dot_nt(grad, weights[i][j][:, at : at + some])
        at += some
    scaled, inverse = normalize([x[...].astype(F32) for x in x_refs])
    grads = norm_back(upstream, scaled, inverse, cut(gain_ref[...], width))
    for i, grad in enumerate(grads):
        add_rows(gain_grad, upstream[i] * scaled[i], i * width)
        add_rows(shift_grad, upstream[i], i * width)
        total = middle_ref[:, i * width : (i + 1) * width] + grad
        o_refs[i][...] = total.astype(o_refs[i].dtype)


def outer_kernel(rights, received, whole_width, a_ref, *refs):
    b_refs, refs = refs[:rights], refs[rights:]
    received, o_refs = refs[:received], refs[received:]
    height, width = o_refs[0].shape
    left = a_ref[...]
    at = 0
    for b_ref in b_refs:
        total = dot_tn(left, b_ref[...])
        where = slice(at, at + total.shape[1])
        for ref in received:
            total += ref[:, where].astype(F32)
        total = total.astype(BF)
        if width < whole_width:
            o_refs[at // width][...] = total
        else:
            for n, o_ref in enumerate(o_refs):
                o_ref[:, where] = total[n * height : (n + 1) * height]
        at = where.stop


def outer(left, rights, left_part, right_part, name, after, received=(), splits=(1, 1)):
    tokens = left.shape[0]
    (li, lw), (ri, rw) = left_part, right_part
    bl, br = min(lw, 1024), 1024 if rw % 1024 == 0 else rw
    down, across = splits
    tile = pl.BlockSpec((bl, br), lambda i, j: (i, j))
    part = pl.BlockSpec((bl // down, br // across), lambda i, j: (i, j))
    spec = pl.BlockSpec((tokens, br // len(rights)), lambda i, j: (0, ri * (rw // br) + j))
    return call(
        partial(outer_kernel, len(rights), len(received), br),
        name,
        (lw // bl, rw // br),
        [(pl.BlockSpec((tokens, bl), lambda i, j: (0, li * (lw // bl) + i)), left)]
        + [(spec, right) for right in rights]
        + [(tile, r) for r in received],
        [(part, (lw // down, rw // across), BF)] * (down * across),
        tokens * lw * rw,
        after,
        weight=LIGHT,
    )


def body(
    block_input,
    image_valid,
    first_gain,
    first_shift,
    attend_weight,
    attend_bias,
    output_weight,
    output_bias,
    second_gain,
    second_shift,
    expand_weight,
    expand_bias,
    reduce_weight,
    reduce_bias,
    output_grad,
):
    rows, cols = lax.axis_size("row"), lax.axis_size("col")
    row_index, col_index = lax.axis_index("row"), lax.axis_index("col")
    local_rows, width = block_input.shape
    local_images = local_rows // SEQ
    images = local_images // rows
    tokens = images * PAD
    hidden_width = expand_weight.shape[1] * cols
    shape = (rows, cols)
    step = (images,)

    local_valid = lax.dynamic_slice_in_dim(image_valid, col_index * local_images, local_images)

    def to_tokens(values, masked, after=()):
        parts = pack_rows(values, row_index, local_valid, masked, after)
        return [shift(part, "row", -s) if s else part for s, part in enumerate(parts)]

    def sent(parts):
        return [shift(a, "row", s) if s else a for s, a in enumerate(parts)]

    features = jnp.stack(
        [first_gain, first_shift, output_bias, second_gain, second_shift, reduce_bias]
    )
    features = jnp.concatenate(gather_blocks(features, "row"), 1).astype(F32)
    first_gain, first_shift, output_bias, second_gain, second_shift, reduce_bias = jnp.split(
        features, 6, 0
    )
    biases = jnp.stack(gather_blocks(jnp.concatenate([attend_bias, expand_bias]), "col"))
    biases = biases.astype(F32)
    pairs = biases[:, : attend_bias.shape[0]].reshape(-1, 2, HD)
    attend_bias = jnp.stack([pairs[:, 0], jnp.zeros_like(pairs[:, 0]), pairs[:, 1]], 1)
    attend_bias = attend_bias.reshape(1, 3 * D)
    expand_bias = biases[:, -expand_bias.shape[0] :].reshape(1, -1)
    valid = lax.dynamic_slice_in_dim(
        image_valid, col_index * local_images + row_index * images, images
    )

    inputs = to_tokens(block_input, False)
    attend_shares, expand_shares = hold(fetch_shares([attend_weight, expand_weight]), inputs[0])
    attend_blocks = gather_shares(attend_weight, attend_shares)
    output_rows = gather_blocks(hold(output_weight, inputs), "row")

    def flat(blocks):
        return [(whole(b), b) for some in blocks for b in some]

    def row_blocks(arrays):
        return [(by_image(width), a) for a in arrays]

    def full(array):
        return (whole(array), array)

    def image(array):
        return (by_image(array.shape[1]), array)

    def out(columns, dtype):
        return (by_image(columns), (tokens, columns), dtype)

    def total(columns):
        return (pl.BlockSpec((1, columns), lambda i: (0, 0)), (1, columns), F32)

    scalars = (pl.BlockSpec(memory_space=pltpu.SMEM), valid)

    first_normed, packed = call(
        partial(project_kernel, shape),
        "project",
        step,
        [full(first_gain), full(first_shift), full(attend_bias)]
        + row_blocks(inputs)
        + flat(attend_blocks),
        [out(D, BF), out(3 * D, BF)],
        tokens * 3 * D * D,
    )
    grads = to_tokens(output_grad, True, (packed,))
    expand_blocks = gather_shares(expand_weight, expand_shares)
    (reduce_shares,) = fetch_shares([hold(reduce_weight, packed)])
    mixed = attend(packed, 0, None, (*expand_shares, *reduce_shares, grads[0]))
    reduce_shares = hold(reduce_shares, mixed)
    mixed = attend(packed, 1, mixed, reduce_shares)
    output_blocks = [gather_blocks(block, "col") for block in hold(output_rows, mixed)]
    middle, second_normed = call(
        partial(output_kernel, shape),
        "output",
        step,
        [full(output_bias), full(second_gain), full(second_shift), image(mixed)]
        + row_blocks(inputs)
        + flat(output_blocks),
        [out(D, F32), out(D, BF)],
        tokens * D * D,
    )
    reduce_blocks = gather_shares(reduce_weight, reduce_shares, second_normed)
    hidden, slope = call(
        partial(expand_kernel, shape),
        "expand",
        step,
        [full(expand_bias), image(second_normed)] + flat(expand_blocks),
        [out(hidden_width, BF), out(hidden_width, BF)],
        tokens * D * hidden_width,
    )
    def add_parts(parts, axis, after=None):
        held = parts[0].astype(F32)
        others = [shift(part, axis, s) for s, part in enumerate(parts) if s]
        for other in others if after is None else hold(others, after):
            held = held + other.astype(F32)
        return held

    def places(left, rights, over_left, j):
        lw, rw = left.shape[1], sum(r.shape[1] for r in rights)
        return ((j, lw // cols), (0, rw)) if over_left else ((0, lw), (j, rw // cols))

    def outer_others(left, rights, over_left, name, after=()):
        received = []
        for j in range(1, cols):
            (block,) = outer(left, rights, *places(left, rights, over_left, j), name, after)
            received.append(shift(block, "col", j))
            after = (block,)
        return received, after

    def outer_own(left, rights, over_left, name, others, after=()):
        received, order = others
        splits = (1, rows) if over_left else (rows, 1)
        where = places(left, rights, over_left, 0)
        return outer(left, rights, *where, name, (*order, *after), received, splits)

    def share_of(held, after=None):
        return add_parts(held, "row", after).astype(BF)

    reduce_others = outer_others(hidden, grads, True, "reduce_outer")
    before_low, reduce_bias_grad, expand_bias_grad = call(
        partial(reduce_back_kernel, shape),
        "reduce_back",
        step,
        [image(slope)] + row_blocks(grads) + flat(reduce_blocks),
        [out(hidden_width, BF), total(D), total(hidden_width)],
        tokens * D * hidden_width,
        reduce_others[1],
        weight=LIGHT,
    )
    reduce_held = outer_own(hidden, grads, True, "reduce_outer", reduce_others, (before_low,))
    reduce_share = share_of(reduce_held)
    expand_others = outer_others(
        second_normed, [before_low], False, "expand_outer", reduce_held[:1]
    )
    middle_grad, mixed_low, second_gain_grad, second_shift_grad, output_bias_grad, *middle_lows = call(
        partial(expand_back_kernel, shape),
        "expand_back",
        step,
        [full(second_gain), image(before_low), image(middle)]
        + row_blocks(grads)
        + flat(expand_blocks)
        + flat(output_blocks),
        [out(D, F32), out(D, BF), total(D), total(D), total(D)] + [out(width, BF)] * rows,
        tokens * D * (hidden_width + D),
        expand_others[1],
        weight=LIGHT,
    )
    expand_held = outer_own(
        second_normed, [before_low], False, "expand_outer", expand_others, (middle_grad,)
    )
    output_others = outer_others(mixed, middle_lows, True, "output_outer", expand_held[:1])
    output_held = outer_own(mixed, middle_lows, True, "output_outer", output_others, (reduce_share,))
    results = call(
        partial(reduce_kernel, shape),
        "reduce",
        step,
        [scalars, full(reduce_bias), image(hidden), image(middle)] + flat(reduce_blocks),
        [out(width, BF)] * rows,
        tokens * D * hidden_width,
        output_held[:1],
        weight=LIGHT,
    )
    block_output = unpack_rows([[part] for part in sent(results)], row_index, BF)

    expand_share = share_of(expand_held, results[0])
    output_share = share_of(output_held, results[0])
    reduce_weight_grad = lax.psum(reduce_share, "dp")
    expand_weight_grad = lax.psum(hold(expand_share, reduce_weight_grad), "dp")
    pairs = 3 * D // (6 * HD) // cols
    counts = [pairs - 2, 1, 1] if pairs > 2 else [pairs]
    packed_lows, held, shares, pair = [], [], [], 0
    ready = results[:1]
    for g, count in enumerate(counts):
        packed_low = None
        for slot in range(count):
            packed_low = attend_back(
                packed, mixed_low, cols, pair, slot, count, packed_low, ready
            )
            ready = (expand_share, output_share) if pair == 0 else ()
            pair += 1
        packed_lows.append(packed_low)
        ready = (expand_weight_grad, *shares[1:]) if pair == pairs else ()
        others = outer_others(first_normed, [packed_low], False, "project_outer", ready)
        held.append(outer_own(first_normed, [packed_low], False, "project_outer", others))
        shares.append(share_of(held[-1]))
        ready = (held[g][0],)
        ready += (shares[g - 1], block_output) if g > 0 else (reduce_weight_grad,)
    output_weight_grad, first_sum = lax.psum(
        hold((output_share, shares[0]), expand_weight_grad), "dp"
    )
    attend_weight_grad = [first_sum]
    if len(shares) > 1:
        attend_weight_grad.append(sum_shares(jnp.concatenate(shares[1:], 1), "dp"))
    attend_weight_grad = jnp.concatenate(attend_weight_grad, 1)

    halves = 2 if images % 2 == 0 else 1
    some = images // halves
    input_grads, sums = [], 0.0
    for half in range(halves):

        def later(array):
            place = half * some
            spec = pl.BlockSpec((PAD, array.shape[1]), lambda i: (i + place, 0))
            return (spec, array)

        def here(dtype):
            return (by_image(width), (some * PAD, width), dtype)

        results = call(
            partial(project_back_kernel, shape, len(counts)),
            "project_back",
            (some,),
            [full(first_gain), later(middle_grad)]
            + [later(p) for p in packed_lows]
            + [later(x) for x in inputs]
            + flat(attend_blocks),
            [here(F32)]
            + [here(BF)] * (rows - 1)
            + [total(D), total(D)]
            + [total(p.shape[1]) for p in packed_lows],
            some * PAD * 3 * D * D,
            ready,
            weight=LIGHT,
        )
        input_grads.append(sent(results[:rows]))
        ready = (results[0], shares[-1])
        packed_sums = [v.reshape(cols, -1, 3, HD) for v in results[rows + 2 :]]
        late = (*results[rows : rows + 2], jnp.concatenate(packed_sums, 1))
        sums = late if half == 0 else jax.tree.map(jnp.add, sums, late)
    input_grad = unpack_rows(list(zip(*hold(input_grads, first_sum))), row_index, F32)
    first_gain_grad, first_shift_grad, packed_sums = sums

    feature_grads = jnp.concatenate(
        [
            first_gain_grad,
            first_shift_grad,
            output_bias_grad,
            second_gain_grad,
            second_shift_grad,
            reduce_bias_grad,
        ]
    )
    attend_bias_grad = jnp.stack([packed_sums[:, :, 0], packed_sums[:, :, 2]], 2)
    attend_bias_grad = attend_bias_grad.reshape(cols, -1)
    bias_grads = jnp.concatenate([attend_bias_grad, expand_bias_grad.reshape(cols, -1)], 1)
    bias_grads = add_parts(list(bias_grads), "col")
    feature_grads = sum_all(feature_grads.reshape(-1), "col")
    small = hold(jnp.concatenate([feature_grads, bias_grads]), input_grads[0][-1])
    small = hold(sum_all(small, "dp"), input_grads[-1][-1])
    feature_grads, bias_grads = small[: 6 * D].reshape(6, D), small[6 * D :]
    feature_grads = add_parts(jnp.split(feature_grads, rows, 1), "row")
    bias_grads = sum_all(bias_grads, "row")
    split = attend_bias_grad.shape[1]
    return (
        block_output,
        input_grad,
        feature_grads[0],
        feature_grads[1],
        attend_weight_grad.astype(F32),
        bias_grads[:split],
        output_weight_grad.astype(F32),
        feature_grads[2],
        feature_grads[3],
        feature_grads[4],
        expand_weight_grad.astype(F32),
        bias_grads[split:],
        reduce_weight_grad.astype(F32),
        feature_grads[5],
    )


def solution(mesh):
    tokens = P(("dp", "col"), "row")
    by_row, by_col = P("row"), P("col")
    up, down = P("row", "col"), P("col", "row")
    params = (by_row, by_row, up, by_col, down, by_row, by_row, by_row, up, by_col, down, by_row)
    return jax.shard_map(
        body,
        mesh=mesh,
        in_specs=(tokens, P("dp")) + params + (tokens,),
        out_specs=(tokens, tokens) + params,
        check_vma=False,
    )
```

```python
from functools import partial

import jax
import jax.numpy as jnp
from jax import lax
from jax.experimental import pallas as pl
from jax.experimental.pallas import tpu as pltpu
from jax.sharding import PartitionSpec as P

D = 1024
HD = 64
SEQ = 577
PAD = 592
EPSILON = 1e-06
BF = jnp.bfloat16
F32 = jnp.float32
LOG2E = 1.4426950408889634
ROOT_HALF = 0.7071067811865476
DENSITY = 0.3989422804014327
KEYS_A = 512
EXPAND_CUT = 1024
LIGHT = 128
PIECES = (slice(0, 304), slice(304, PAD))
QUERY_CUTS = (0, 208, 400, PAD)
MEBI = 1 << 20


def dot_nn(left, right):
    return lax.dot_general(left, right, (((1,), (0,)), ((), ())), preferred_element_type=F32)


def dot_nt(left, right):
    return lax.dot_general(left, right, (((1,), (1,)), ((), ())), preferred_element_type=F32)


def dot_tn(left, right):
    return lax.dot_general(left, right, (((0,), (0,)), ((), ())), preferred_element_type=F32)


def whole(array):
    return pl.BlockSpec(array.shape, lambda *_: (0,) * array.ndim, pipeline_mode=pl.Buffered(1))


def by_image(width):
    return pl.BlockSpec((PAD, width), lambda i: (i, 0))


def call(kernel, name, grid, operands, outputs, macs, after=(), into=None, weight=1):
    if into is not None:
        after = (into, *after)
    size = sum(a.size * a.dtype.itemsize for _, a in operands)
    size += sum(jnp.dtype(t).itemsize * s[0] * s[1] for _, s, t in outputs)
    used = len(operands)

    def body_of(*refs):
        kernel(*refs[:used], *refs[used + len(after) :])

    return pl.pallas_call(
        body_of,
        grid=grid,
        in_specs=[s for s, _ in operands] + [pl.BlockSpec(memory_space=pl.ANY)] * len(after),
        out_specs=[s for s, _, _ in outputs],
        out_shape=[jax.ShapeDtypeStruct(s, t) for _, s, t in outputs],
        compiler_params=pltpu.CompilerParams(vmem_limit_bytes=60 * MEBI),
        cost_estimate=pl.CostEstimate(flops=2 * macs // weight, bytes_accessed=size // weight, transcendentals=0),
        input_output_aliases={} if into is None else {used: 0},
        name=name,
    )(*[a for _, a in operands], *after)


def shift(values, axis, step):
    size = lax.axis_size(axis)
    return lax.ppermute(values, axis, [(i, (i + step) % size) for i in range(size)])


def gather_blocks(block, axis):
    return [block] + [shift(block, axis, -s) for s in range(1, lax.axis_size(axis))]


def gather_weight(weight):
    return [gather_blocks(block, "col") for block in gather_blocks(weight, "row")]


def fetch_shares(weights):
    place = lax.axis_index("dp")
    depths = [w.shape[0] // lax.axis_size("dp") for w in weights]
    shares = [lax.dynamic_slice_in_dim(w, place * d, d) for w, d in zip(weights, depths)]
    widths = [w.shape[1] for w in weights]
    fetched = gather_blocks(jnp.concatenate(shares, 1), "row")[1:]
    ends = [sum(widths[: n + 1]) for n in range(len(widths))]
    return [[f[:, end - w : end] for f in fetched] for end, w in zip(ends, widths)]


def gather_shares(weight, shares, after=None):
    blocks = [lax.all_gather(s, "dp", axis=0, tiled=True) for s in shares]
    blocks = [weight] + (blocks if after is None else hold(blocks, after))
    return [gather_blocks(block, "col") for block in blocks]


def hold(values, after):
    return lax.optimization_barrier((values, after))[0]


def swap(values, axis, step):
    return lax.ppermute(values, axis, [(i, i ^ step) for i in range(lax.axis_size(axis))])


def steps_of(axis):
    steps = [1]
    while steps[-1] * 2 < lax.axis_size(axis):
        steps.append(steps[-1] * 2)
    return steps


def sum_all(values, axis):
    for step in steps_of(axis):
        values = values + swap(values, axis, step)
    return values


def halve(values, axis, step):
    half = values.shape[0] // 2
    bit = lax.axis_index(axis) // step % 2
    keep = lax.dynamic_slice_in_dim(values, bit * half, half)
    give = lax.dynamic_slice_in_dim(values, (1 - bit) * half, half)
    return (keep.astype(F32) + swap(give, axis, step).astype(F32)).astype(BF)


def join(values, axis, step):
    other = swap(values, axis, step)
    low = lax.axis_index(axis) // step % 2 == 0
    return jnp.where(low, jnp.concatenate([values, other]), jnp.concatenate([other, values]))


def sum_shares(values, axis):
    for step in steps_of(axis):
        values = halve(values, axis, step)
    for step in reversed(steps_of(axis)):
        values = join(values, axis, step)
    return values


def pack_kernel(masked, place_ref, valid_ref, x_ref, *refs):
    o_refs = refs[-lax.axis_size("row") :]
    images = o_refs[0].shape[0] // PAD
    for place in range(len(o_refs)):

        @pl.when(place_ref[0] == place)
        def _(place=place):
            for s, o_ref in enumerate(o_refs):
                at = (place - s) % len(o_refs) * images
                for i in range(images):
                    rows = x_ref[(at + i) * SEQ : (at + i + 1) * SEQ]
                    if masked:
                        rows = (rows.astype(F32) * valid_ref[at + i].astype(F32)).astype(rows.dtype)
                    o_ref[i * PAD : i * PAD + SEQ] = rows
                    rest = (PAD - SEQ, x_ref.shape[1])
                    o_ref[i * PAD + SEQ : (i + 1) * PAD] = jnp.zeros(rest, x_ref.dtype)


def pack_rows(values, place, valid, masked, after=()):
    rows, width = values.shape
    parts = lax.axis_size("row")
    vmem, smem = pl.BlockSpec(memory_space=pltpu.VMEM), pl.BlockSpec(memory_space=pltpu.SMEM)
    part = jax.ShapeDtypeStruct((rows // SEQ // parts * PAD, width), values.dtype)
    return pl.pallas_call(
        partial(pack_kernel, masked),
        in_specs=[smem, smem, vmem] + [pl.BlockSpec(memory_space=pl.ANY)] * len(after),
        out_specs=[vmem] * parts,
        out_shape=[part] * parts,
        compiler_params=pltpu.CompilerParams(vmem_limit_bytes=60 * MEBI),
        cost_estimate=pl.CostEstimate(flops=0, bytes_accessed=values.size // 8, transcendentals=0),
        name="pack_rows",
    )(place.reshape(1), valid, values, *after)


def unpack_kernel(counts, place_ref, *refs):
    o_ref = refs[-1]
    for place in range(len(counts)):

        @pl.when(place_ref[0] == place)
        def _(place=place):
            n = 0
            for s, some in enumerate(counts):
                at = (place - s) % len(counts) * sum(some)
                for count in some:
                    for i in range(count):
                        rows = refs[n][i * PAD : i * PAD + SEQ].astype(o_ref.dtype)
                        o_ref[at * SEQ : (at + 1) * SEQ] = rows
                        at += 1
                    n += 1


def unpack_rows(parts, place, dtype):
    counts = tuple(tuple(a.shape[0] // PAD for a in some) for some in parts)
    arrays = [a for some in parts for a in some]
    vmem = pl.BlockSpec(memory_space=pltpu.VMEM)
    return pl.pallas_call(
        partial(unpack_kernel, counts),
        in_specs=[pl.BlockSpec(memory_space=pltpu.SMEM)] + [vmem] * len(arrays),
        out_specs=vmem,
        out_shape=jax.ShapeDtypeStruct(
            (sum(map(sum, counts)) * SEQ, arrays[0].shape[1]), dtype
        ),
        compiler_params=pltpu.CompilerParams(vmem_limit_bytes=60 * MEBI),
        cost_estimate=pl.CostEstimate(
            flops=0, bytes_accessed=arrays[0].size // 8, transcendentals=0
        ),
        name="unpack_rows",
    )(place.reshape(1), *arrays)


def row_mean(blocks):
    return sum(jnp.sum(b, 1, keepdims=True) for b in blocks) / (len(blocks) * blocks[0].shape[1])


def normalize(blocks):
    center = row_mean(blocks)
    inverse = lax.rsqrt(row_mean([b * b for b in blocks]) - center * center + EPSILON)
    return [(b - center) * inverse for b in blocks], inverse


def norm_back(upstream, scaled, inverse, gains):
    grads = [u * g for u, g in zip(upstream, gains)]
    plain = row_mean(grads)
    cross = row_mean([g * x for g, x in zip(grads, scaled)])
    return [inverse * (g - plain - x * cross) for g, x in zip(grads, scaled)]


def cut(values, width):
    return [values[:, at : at + width] for at in range(0, values.shape[1], width)]


def add_rows(ref, values, at=0):
    ref[:, at : at + values.shape[1]] += jnp.sum(values, 0, keepdims=True)


def grid_of(refs, shape):
    outer, inner = shape
    return [refs[i * inner : (i + 1) * inner] for i in range(outer)]


def project_kernel(shape, gain_ref, shift_ref, bias_ref, *refs):
    rows, cols = shape
    x_refs, weights = refs[:rows], grid_of(refs[rows : rows + rows * cols], shape)
    normed_ref, packed_ref = refs[rows + rows * cols :]
    width, block = weights[0][0].shape
    gains, shifts = cut(gain_ref[...], width), cut(shift_ref[...], width)
    for some in PIECES:
        scaled, _ = normalize([x[some, :].astype(F32) for x in x_refs])
        normed = [(x * g + b).astype(BF) for x, g, b in zip(scaled, gains, shifts)]
        for i, n in enumerate(normed):
            normed_ref[some, i * width : (i + 1) * width] = n
        for j in range(cols):
            total = sum(dot_nn(n, weights[i][j][...]) for i, n in enumerate(normed))
            where = slice(j * block, (j + 1) * block)
            packed_ref[some, where] = (total + bias_ref[:, where]).astype(BF)


def swap_halves(values):
    return jnp.concatenate([values[:, HD:], values[:, :HD]], 1)


def attend_kernel(p_ref, o_ref):
    first, second, third = p_ref[:, :128], p_ref[:, 128:256], p_ref[:, 256:]
    low = lax.broadcasted_iota(jnp.int32, (1, 128), 1) < HD
    zero, one = jnp.zeros((), BF), jnp.ones((), BF)
    queries = (jnp.where(low, first, zero), jnp.where(low, swap_halves(second), zero))
    keys = (swap_halves(first), third)
    values = (jnp.where(low, second, one), jnp.where(low, one, third))
    scale = HD**-0.5 * LOG2E
    keep = lax.broadcasted_iota(jnp.int32, (1, PAD - KEYS_A), 1) < SEQ - KEYS_A
    units = [(slice(*cut), h) for cut in zip(QUERY_CUTS, QUERY_CUTS[1:]) for h in range(2)]
    scores = [
        (dot_nt(queries[h][some], keys[h][:KEYS_A]), dot_nt(queries[h][some], keys[h][KEYS_A:]))
        for some, h in units
    ]
    weights = []
    for sa, sb in scores:
        sb = jnp.where(keep, sb, -1e30)
        top = jnp.maximum(jnp.max(sa, 1, keepdims=True), jnp.max(sb, 1, keepdims=True)) * scale
        weights.append([jnp.exp2(v * scale - top).astype(BF) for v in (sa, sb)])
    outs = [
        dot_nn(pa, values[h][:KEYS_A]) + dot_nn(pb, values[h][KEYS_A:])
        for (_, h), (pa, pb) in zip(units, weights)
    ]
    for n in range(0, len(units), 2):
        mixed, totals = jnp.where(low, *outs[n : n + 2]), jnp.where(low, *outs[n : n + 2][::-1])
        o_ref[units[n][0], :] = (mixed / swap_halves(totals)).astype(BF)


def attend(packed, first, some, into, after):
    tokens, width = packed.shape
    pairs = width // (6 * HD)
    return call(
        attend_kernel,
        "attend",
        (some, tokens // PAD),
        [(pl.BlockSpec((PAD, 6 * HD), lambda h, i: (i, first + h)), packed)],
        [
            (
                pl.BlockSpec((PAD, 2 * HD), lambda h, i: (i, first + h)),
                (tokens, pairs * 2 * HD),
                BF,
            )
        ],
        tokens * PAD * some * 2 * HD * 5,
        after,
        into,
    )[0]


def attend_back_kernel(p_ref, g_ref, o_ref):
    first, second, third = p_ref[:, :128], p_ref[:, 128:256], p_ref[:, 256:]
    grad = g_ref[...]
    low = lax.broadcasted_iota(jnp.int32, (1, 128), 1) < HD
    zero = jnp.zeros((), BF)
    turned = [swap_halves(v) for v in (first, second, third)]
    queries = (jnp.where(low, first, zero), jnp.where(low, turned[1], zero))
    keys, values = (turned[0], third), (second, third)
    grads = (jnp.where(low, grad, zero), jnp.where(low, zero, grad))
    query_right = (turned[0], turned[1])
    key_right = (turned[0], turned[2])
    scale = HD**-0.5
    edge = PAD - 16
    keep = lax.broadcasted_iota(jnp.int32, (PAD - edge, 1), 0) < SEQ - edge
    units = [(slice(at, min(PAD, at + 256)), h) for at in range(0, PAD, 256) for h in range(2)]
    products = [
        (dot_nt(keys[h], queries[h][some]), dot_nt(values[h], grads[h][some])) for some, h in units
    ]
    lows = []
    for scores, weight_grad in products:
        sa, sb = scores[:edge], jnp.where(keep, scores[edge:], -1e30)
        top = jnp.maximum(jnp.max(sa, 0, keepdims=True), jnp.max(sb, 0, keepdims=True))
        top = top * (scale * LOG2E)
        weights = jnp.concatenate([jnp.exp2(s * (scale * LOG2E) - top) for s in (sa, sb)], 0)
        share = 1.0 / jnp.sum(weights, 0, keepdims=True)
        product = weights * weight_grad
        row_dot = jnp.sum(product, 0, keepdims=True) * share
        score_low = (product - weights * row_dot) * share
        lows.append(((weights * share).astype(BF), score_low.astype(BF)))
    value_grad, key_grad, query_grad = [0.0, 0.0], [0.0, 0.0], [[], []]
    for (some, h), (weights, score_low) in zip(units, lows):
        value_grad[h] += dot_nn(weights, grad[some])
        key_grad[h] += dot_nn(score_low, query_right[h][some])
        query_grad[h].append(dot_tn(key_right[h], score_low).T)
    query_grad = [jnp.concatenate(q, 0) for q in query_grad]
    o_ref[:, :128] = (jnp.where(low, query_grad[0], key_grad[0]) * scale).astype(BF)
    o_ref[:, 128:256] = jnp.where(low, value_grad[0], query_grad[1] * scale).astype(BF)
    o_ref[:, 256:] = jnp.where(low, key_grad[1] * scale, value_grad[1]).astype(BF)


def attend_back(packed, grad, cols, pair, slot, slots, into, after):
    tokens, width = packed.shape
    block = width // (6 * HD) // cols
    return call(
        attend_back_kernel,
        "attend_back",
        (cols, tokens // PAD),
        [
            (pl.BlockSpec((PAD, 6 * HD), lambda j, i: (i, j * block + pair)), packed),
            (pl.BlockSpec((PAD, 2 * HD), lambda j, i: (i, j * block + pair)), grad),
        ],
        [
            (
                pl.BlockSpec((PAD, 6 * HD), lambda j, i: (i, j * slots + slot)),
                (tokens, cols * slots * 6 * HD),
                BF,
            )
        ],
        tokens * PAD * cols * 2 * HD * 12,
        after,
        into,
        LIGHT,
    )[0]


def output_kernel(shape, bias_ref, gain_ref, shift_ref, mixed_ref, *refs):
    rows, cols = shape
    x_refs, weights = refs[:rows], grid_of(refs[rows : rows + rows * cols], shape)
    middle_ref, normed_ref = refs[rows + rows * cols :]
    block, width = weights[0][0].shape
    spans = [slice(i * width, (i + 1) * width) for i in range(rows)]
    totals = []
    for some in PIECES:
        mixed = cut(mixed_ref[some, :], block)
        totals.append(
            [
                sum(dot_nn(m, weights[i][j][...]) for j, m in enumerate(mixed))
                for i in range(rows)
            ]
        )
    for some, total in zip(PIECES, totals):
        middle = []
        for i, where in enumerate(spans):
            middle.append(x_refs[i][some, :].astype(F32) + total[i] + bias_ref[:, where])
            middle_ref[some, where] = middle[-1]
        scaled, _ = normalize(middle)
        for x, where in zip(scaled, spans):
            normed = x * gain_ref[:, where] + shift_ref[:, where]
            normed_ref[some, where] = normed.astype(BF)


def expand_kernel(shape, bias_ref, normed_ref, *refs):
    rows, cols = shape
    weights = grid_of(refs[: rows * cols], shape)
    hidden_ref, slope_ref = refs[rows * cols :]
    depth, block = weights[0][0].shape
    cuts = [
        (some, j, at)
        for some in PIECES
        for j in range(cols)
        for at in range(0, block, min(block, EXPAND_CUT))
    ]
    normed = {some.start: cut(normed_ref[some, :], depth) for some in PIECES}
    wide = min(block, EXPAND_CUT)
    totals = [
        sum(
            dot_nn(n, weights[i][j][:, at : at + wide])
            for i, n in enumerate(normed[some.start])
        )
        for some, j, at in cuts
    ]
    for (some, j, at), total in zip(cuts, totals):
        where = slice(j * block + at, j * block + at + wide)
        before = total + bias_ref[:, where]
        below = 0.5 + 0.5 * lax.erf(before * ROOT_HALF)
        hidden_ref[some, where] = (before * below).astype(BF)
        density = jnp.exp2(before * before * (-0.5 * LOG2E)) * DENSITY
        slope_ref[some, where] = (below + before * density).astype(BF)


def reduce_kernel(shape, valid_ref, bias_ref, hidden_ref, middle_ref, *refs):
    rows, cols = shape
    weights, o_refs = grid_of(refs[: rows * cols], shape), refs[rows * cols :]
    block, width = weights[0][0].shape
    valid = valid_ref[pl.program_id(0)].astype(F32)
    for i in range(rows):
        total = sum(
            dot_nn(hidden_ref[:, j * block : (j + 1) * block], weights[i][j][...])
            for j in range(cols)
        )
        where = slice(i * width, (i + 1) * width)
        o_refs[i][...] = ((middle_ref[:, where] + total + bias_ref[:, where]) * valid).astype(BF)


def reduce_back_kernel(shape, slope_ref, *refs):
    rows, cols = shape
    g_refs, weights = refs[:rows], grid_of(refs[rows : rows + rows * cols], shape)
    before_ref, reduce_bias_ref, expand_bias_ref = refs[rows + rows * cols :]

    @pl.when(pl.program_id(0) == 0)
    def _():
        reduce_bias_ref[...] = jnp.zeros_like(reduce_bias_ref)
        expand_bias_ref[...] = jnp.zeros_like(expand_bias_ref)

    block, width = weights[0][0].shape
    lows = [g[...] for g in g_refs]
    for i, low in enumerate(lows):
        add_rows(reduce_bias_ref, low.astype(F32), i * width)
    for j in range(cols):
        total = sum(dot_nt(low, weights[i][j][...]) for i, low in enumerate(lows))
        where = slice(j * block, (j + 1) * block)
        total = total * slope_ref[:, where].astype(F32)
        add_rows(expand_bias_ref, total, j * block)
        before_ref[:, where] = total.astype(BF)


def expand_back_kernel(shape, gain_ref, before_ref, middle_ref, *refs):
    rows, cols = shape
    g_refs, refs = refs[:rows], refs[rows:]
    count = rows * cols
    expand, output = grid_of(refs[:count], shape), grid_of(refs[count : 2 * count], shape)
    refs = refs[2 * count :]
    middle_grad_ref, mixed_low_ref, gain_grad, shift_grad, bias_grad = refs[:5]
    low_refs = refs[5:]

    @pl.when(pl.program_id(0) == 0)
    def _():
        for ref in (gain_grad, shift_grad, bias_grad):
            ref[...] = jnp.zeros_like(ref)

    width, block = expand[0][0].shape
    spans = [slice(i * width, (i + 1) * width) for i in range(rows)]
    heads = output[0][0].shape[0]
    upstreams = [
        [
            sum(
                dot_nt(before_ref[some, j * block : (j + 1) * block], expand[i][j][...])
                for j in range(cols)
            )
            for i in range(rows)
        ]
        for some in PIECES
    ]
    for some, upstream in zip(PIECES, upstreams):
        scaled, inverse = normalize(cut(middle_ref[some, :], width))
        parts = norm_back(upstream, scaled, inverse, cut(gain_ref[...], width))
        lows = []
        for i, part in enumerate(parts):
            add_rows(gain_grad, upstream[i] * scaled[i], i * width)
            add_rows(shift_grad, upstream[i], i * width)
            grad = g_refs[i][some, :].astype(F32) + part
            add_rows(bias_grad, grad, i * width)
            middle_grad_ref[some, spans[i]] = grad
            lows.append(grad.astype(BF))
            low_refs[i][some, :] = lows[-1]
        for j in range(cols):
            total = sum(dot_nt(low, output[i][j][...]) for i, low in enumerate(lows))
            mixed_low_ref[some, j * heads : (j + 1) * heads] = total.astype(BF)


def project_back_kernel(shape, parts, gain_ref, middle_ref, *refs):
    rows, cols = shape
    packed, refs = refs[:parts], refs[parts:]
    x_refs, weights = refs[:rows], grid_of(refs[rows : rows + rows * cols], shape)
    refs = refs[rows + rows * cols :]
    o_refs, (gain_grad, shift_grad), bias_grads = refs[:rows], refs[rows : rows + 2], refs[rows + 2 :]

    @pl.when(pl.program_id(0) == 0)
    def _():
        for ref in refs[rows:]:
            ref[...] = jnp.zeros_like(ref)

    width = weights[0][0].shape[0]
    for p in range(parts):
        add_rows(bias_grads[p], packed[p][...].astype(F32))
    upstreams = []
    for piece in PIECES:
        upstream = [0.0] * rows
        at = 0
        for p in range(parts):
            some = packed[p].shape[1] // cols
            for j in range(cols):
                grad = packed[p][piece, j * some : (j + 1) * some]
                for i in range(rows):
                    upstream[i] += dot_nt(grad, weights[i][j][:, at : at + some])
            at += some
        upstreams.append(upstream)
    for piece, upstream in zip(PIECES, upstreams):
        scaled, inverse = normalize([x[piece, :].astype(F32) for x in x_refs])
        grads = norm_back(upstream, scaled, inverse, cut(gain_ref[...], width))
        for i, grad in enumerate(grads):
            add_rows(gain_grad, upstream[i] * scaled[i], i * width)
            add_rows(shift_grad, upstream[i], i * width)
            total = middle_ref[piece, i * width : (i + 1) * width] + grad
            o_refs[i][piece, :] = total.astype(o_refs[i].dtype)


def outer_kernel(rights, received, whole_width, a_ref, *refs):
    b_refs, refs = refs[:rights], refs[rights:]
    received, o_refs = refs[:received], refs[received:]
    height, width = o_refs[0].shape
    left = a_ref[...]
    at = 0
    for b_ref in b_refs:
        total = dot_tn(left, b_ref[...])
        where = slice(at, at + total.shape[1])
        for ref in received:
            total += ref[:, where].astype(F32)
        total = total.astype(BF)
        if width < whole_width:
            o_refs[at // width][...] = total
        else:
            for n, o_ref in enumerate(o_refs):
                o_ref[:, where] = total[n * height : (n + 1) * height]
        at = where.stop


def outer(left, rights, left_part, right_part, name, after, received=(), splits=(1, 1)):
    tokens = left.shape[0]
    (li, lw), (ri, rw) = left_part, right_part
    bl, br = min(lw, 1024), 1024 if rw % 1024 == 0 else rw
    down, across = splits
    tile = pl.BlockSpec((bl, br), lambda i, j: (i, j))
    part = pl.BlockSpec((bl // down, br // across), lambda i, j: (i, j))
    spec = pl.BlockSpec((tokens, br // len(rights)), lambda i, j: (0, ri * (rw // br) + j))
    return call(
        partial(outer_kernel, len(rights), len(received), br),
        name,
        (lw // bl, rw // br),
        [(pl.BlockSpec((tokens, bl), lambda i, j: (0, li * (lw // bl) + i)), left)]
        + [(spec, right) for right in rights]
        + [(tile, r) for r in received],
        [(part, (lw // down, rw // across), BF)] * (down * across),
        tokens * lw * rw,
        after,
        weight=1 if name in ("reduce_outer", "expand_outer") else LIGHT,
    )


def body(
    block_input,
    image_valid,
    first_gain,
    first_shift,
    attend_weight,
    attend_bias,
    output_weight,
    output_bias,
    second_gain,
    second_shift,
    expand_weight,
    expand_bias,
    reduce_weight,
    reduce_bias,
    output_grad,
):
    rows, cols = lax.axis_size("row"), lax.axis_size("col")
    row_index, col_index = lax.axis_index("row"), lax.axis_index("col")
    local_rows, width = block_input.shape
    local_images = local_rows // SEQ
    images = local_images // rows
    tokens = images * PAD
    hidden_width = expand_weight.shape[1] * cols
    shape = (rows, cols)
    step = (images,)

    local_valid = lax.dynamic_slice_in_dim(image_valid, col_index * local_images, local_images)

    def to_tokens(values, masked, after=()):
        parts = pack_rows(values, row_index, local_valid, masked, after)
        return [shift(part, "row", -s) if s else part for s, part in enumerate(parts)]

    def sent(parts):
        return [shift(a, "row", s) if s else a for s, a in enumerate(parts)]

    features = jnp.stack(
        [first_gain, first_shift, output_bias, second_gain, second_shift, reduce_bias]
    )
    features = jnp.concatenate(gather_blocks(features, "row"), 1).astype(F32)
    first_gain, first_shift, output_bias, second_gain, second_shift, reduce_bias = jnp.split(
        features, 6, 0
    )
    biases = jnp.stack(gather_blocks(jnp.concatenate([attend_bias, expand_bias]), "col"))
    biases = biases.astype(F32)
    pairs = biases[:, : attend_bias.shape[0]].reshape(-1, 2, HD)
    attend_bias = jnp.stack([pairs[:, 0], jnp.zeros_like(pairs[:, 0]), pairs[:, 1]], 1)
    attend_bias = attend_bias.reshape(1, 3 * D)
    expand_bias = biases[:, -expand_bias.shape[0] :].reshape(1, -1)
    valid = lax.dynamic_slice_in_dim(
        image_valid, col_index * local_images + row_index * images, images
    )

    inputs = to_tokens(block_input, False)
    attend_shares, expand_shares = hold(fetch_shares([attend_weight, expand_weight]), inputs[0])
    attend_blocks = gather_shares(attend_weight, attend_shares)
    output_rows = gather_blocks(hold(output_weight, inputs), "row")

    def flat(blocks):
        return [(whole(b), b) for some in blocks for b in some]

    def row_blocks(arrays):
        return [(by_image(width), a) for a in arrays]

    def full(array):
        return (whole(array), array)

    def image(array):
        return (by_image(array.shape[1]), array)

    def out(columns, dtype):
        return (by_image(columns), (tokens, columns), dtype)

    def total(columns):
        return (pl.BlockSpec((1, columns), lambda i: (0, 0)), (1, columns), F32)

    scalars = (pl.BlockSpec(memory_space=pltpu.SMEM), valid)

    first_normed, packed = call(
        partial(project_kernel, shape),
        "project",
        step,
        [full(first_gain), full(first_shift), full(attend_bias)]
        + row_blocks(inputs)
        + flat(attend_blocks),
        [out(D, BF), out(3 * D, BF)],
        tokens * 3 * D * D,
    )
    grads = to_tokens(output_grad, True, (packed,))
    (reduce_shares,) = fetch_shares([hold(reduce_weight, packed)])
    pairs = packed.shape[1] // (6 * HD)
    mixed = attend(packed, 0, pairs // 4, None, (*expand_shares, *reduce_shares, grads[0]))
    expand_blocks = gather_shares(expand_weight, expand_shares, mixed)
    reduce_shares = hold(reduce_shares, mixed)
    mixed = attend(packed, pairs // 4, pairs - pairs // 4, mixed, reduce_shares)
    output_blocks = [gather_blocks(block, "col") for block in hold(output_rows, mixed)]
    middle, second_normed = call(
        partial(output_kernel, shape),
        "output",
        step,
        [full(output_bias), full(second_gain), full(second_shift), image(mixed)]
        + row_blocks(inputs)
        + flat(output_blocks),
        [out(D, F32), out(D, BF)],
        tokens * D * D,
    )
    reduce_blocks = gather_shares(reduce_weight, reduce_shares, second_normed)
    hidden, slope = call(
        partial(expand_kernel, shape),
        "expand",
        step,
        [full(expand_bias), image(second_normed)] + flat(expand_blocks),
        [out(hidden_width, BF), out(hidden_width, BF)],
        tokens * D * hidden_width,
        (*reduce_blocks[0][1:], *reduce_blocks[-1][:1]),
    )
    def add_parts(parts, axis, after=None):
        held = parts[0].astype(F32)
        others = [shift(part, axis, s) for s, part in enumerate(parts) if s]
        for other in others if after is None else hold(others, after):
            held = held + other.astype(F32)
        return held

    def places(left, rights, over_left, j):
        lw, rw = left.shape[1], sum(r.shape[1] for r in rights)
        return ((j, lw // cols), (0, rw)) if over_left else ((0, lw), (j, rw // cols))

    def outer_others(left, rights, over_left, name, after=()):
        received = []
        for j in range(1, cols):
            (block,) = outer(left, rights, *places(left, rights, over_left, j), name, after)
            received.append(shift(block, "col", j))
            after = (block,)
        return received, after

    def outer_own(left, rights, over_left, name, others, after=()):
        received, order = others
        splits = (1, rows) if over_left else (rows, 1)
        where = places(left, rights, over_left, 0)
        return outer(left, rights, *where, name, (*order, *after), received, splits)

    def share_of(held, after=None):
        received = [shift(part, "row", s) for s, part in enumerate(held) if s]
        total = held[0].astype(F32)
        for part in received if after is None else hold(received, after):
            total = total + part.astype(F32)
        return total.astype(BF), received

    reduce_others = outer_others(hidden, grads, True, "reduce_outer", reduce_blocks[-1][:1])
    before_low, reduce_bias_grad, expand_bias_grad = call(
        partial(reduce_back_kernel, shape),
        "reduce_back",
        step,
        [image(slope)] + row_blocks(grads) + flat(reduce_blocks),
        [out(hidden_width, BF), total(D), total(hidden_width)],
        tokens * D * hidden_width,
        reduce_others[1],
        weight=LIGHT,
    )
    reduce_held = outer_own(hidden, grads, True, "reduce_outer", reduce_others, (before_low,))
    reduce_share, reduce_received = share_of(reduce_held)
    expand_others = outer_others(
        second_normed, [before_low], False, "expand_outer", reduce_held[:1]
    )
    middle_grad, mixed_low, second_gain_grad, second_shift_grad, output_bias_grad, *middle_lows = call(
        partial(expand_back_kernel, shape),
        "expand_back",
        step,
        [full(second_gain), image(before_low), image(middle)]
        + row_blocks(grads)
        + flat(expand_blocks)
        + flat(output_blocks),
        [out(D, F32), out(D, BF), total(D), total(D), total(D)] + [out(width, BF)] * rows,
        tokens * D * (hidden_width + D),
        expand_others[1],
        weight=LIGHT,
    )
    expand_held = outer_own(
        second_normed, [before_low], False, "expand_outer", expand_others, (middle_grad, *reduce_received)
    )
    output_others = outer_others(mixed, middle_lows, True, "output_outer", expand_held[:1])
    output_held = outer_own(mixed, middle_lows, True, "output_outer", output_others)
    results = call(
        partial(reduce_kernel, shape),
        "reduce",
        step,
        [scalars, full(reduce_bias), image(hidden), image(middle)] + flat(reduce_blocks),
        [out(width, BF)] * rows,
        tokens * D * hidden_width,
        output_held[:1],
        weight=LIGHT,
    )
    block_output = unpack_rows([[part] for part in sent(results)], row_index, BF)

    reduce_weight_grad = lax.psum(reduce_share, "dp")
    expand_share, _ = share_of(expand_held, reduce_weight_grad)
    output_share, output_received = share_of(output_held)
    expand_weight_grad, output_weight_grad = lax.psum((expand_share, output_share), "dp")
    pairs = 3 * D // (6 * HD) // cols
    counts = [pairs - 2, 1, 1] if pairs > 2 else [pairs]
    packed_lows, held, shares, halved, arrived, pair = [], [], [], [], (), 0
    ready = results[:1]
    for g, count in enumerate(counts):
        packed_low = None
        for slot in range(count):
            packed_low = attend_back(
                packed, mixed_low, cols, pair, slot, count, packed_low, ready
            )
            ready = output_received if pair == 0 else ()
            pair += 1
        packed_lows.append(packed_low)
        last, own_last = (reduce_weight_grad,) if g == 0 else (), ()
        if g == 2:
            last, own_last = (expand_weight_grad, halved[1]), (halved[2],)
        others = outer_others(first_normed, [packed_low], False, "project_outer", last)
        held.append(outer_own(first_normed, [packed_low], False, "project_outer", others, own_last))
        ready = (held[g][0],)
        if g == 0:
            shares.append(share_of(held[0])[0])
            halved.append(shares[0])
            for hop in steps_of("dp"):
                halved.append(halve(halved[-1], "dp", hop))
        elif g == 1:
            shares.append(share_of(held[1])[0])
            ready += (block_output, shares[0])
        else:
            ready += (halved[3],)
    joined = halved[-1:]
    for hop in reversed(steps_of("dp")):
        joined.append(join(joined[-1], "dp", hop))

    halves = 2 if images % 2 == 0 else 1
    some = images // halves
    input_grads, sums = [], 0.0
    for half in range(halves):

        def later(array):
            place = half * some
            spec = pl.BlockSpec((PAD, array.shape[1]), lambda i: (i + place, 0))
            return (spec, array)

        def here(dtype):
            return (by_image(width), (some * PAD, width), dtype)

        results = call(
            partial(project_back_kernel, shape, len(counts)),
            "project_back",
            (some,),
            [full(first_gain), later(middle_grad)]
            + [later(p) for p in packed_lows]
            + [later(x) for x in inputs]
            + flat(attend_blocks),
            [here(F32)]
            + [here(BF)] * (rows - 1)
            + [total(D), total(D)]
            + [total(p.shape[1]) for p in packed_lows],
            some * PAD * 3 * D * D,
            ready,
            weight=LIGHT,
        )
        input_grads.append(sent(results[:rows]))
        if half == 0 and len(counts) > 1:
            share, arrived = share_of(held[-1], results[0])
            shares.append(share)
        ready = (results[0], *arrived, joined[1])
        packed_sums = [v.reshape(cols, -1, 3, HD) for v in results[rows + 2 :]]
        late = (*results[rows : rows + 2], jnp.concatenate(packed_sums, 1))
        sums = late if half == 0 else jax.tree.map(jnp.add, sums, late)
    input_grad = unpack_rows(list(zip(*input_grads)), row_index, F32)
    first_gain_grad, first_shift_grad, packed_sums = sums
    attend_weight_grad = joined[-1:]
    if len(shares) > 1:
        attend_weight_grad.append(sum_shares(jnp.concatenate(shares[1:], 1), "dp"))
    attend_weight_grad = jnp.concatenate(attend_weight_grad, 1)

    feature_grads = jnp.concatenate(
        [
            first_gain_grad,
            first_shift_grad,
            output_bias_grad,
            second_gain_grad,
            second_shift_grad,
            reduce_bias_grad,
        ]
    )
    attend_bias_grad = jnp.stack([packed_sums[:, :, 0], packed_sums[:, :, 2]], 2)
    attend_bias_grad = attend_bias_grad.reshape(cols, -1)
    bias_grads = jnp.concatenate([attend_bias_grad, expand_bias_grad.reshape(cols, -1)], 1)
    bias_grads = add_parts(list(bias_grads), "col")
    feature_grads = sum_all(feature_grads.reshape(-1), "col")
    small = hold(jnp.concatenate([feature_grads, bias_grads]), input_grads[0][-1])
    small = hold(sum_all(small, "dp"), input_grads[-1][-1])
    feature_grads, bias_grads = small[: 6 * D].reshape(6, D), small[6 * D :]
    feature_grads = add_parts(jnp.split(feature_grads, rows, 1), "row")
    bias_grads = sum_all(bias_grads, "row")
    split = attend_bias_grad.shape[1]
    return (
        block_output,
        input_grad,
        feature_grads[0],
        feature_grads[1],
        attend_weight_grad.astype(F32),
        bias_grads[:split],
        output_weight_grad.astype(F32),
        feature_grads[2],
        feature_grads[3],
        feature_grads[4],
        expand_weight_grad.astype(F32),
        bias_grads[split:],
        reduce_weight_grad.astype(F32),
        feature_grads[5],
    )


def solution(mesh):
    tokens = P(("dp", "col"), "row")
    by_row, by_col = P("row"), P("col")
    up, down = P("row", "col"), P("col", "row")
    params = (by_row, by_row, up, by_col, down, by_row, by_row, by_row, up, by_col, down, by_row)
    return jax.shard_map(
        body,
        mesh=mesh,
        in_specs=(tokens, P("dp")) + params + (tokens,),
        out_specs=(tokens, tokens) + params,
        check_vma=False,
    )
```

```python
from functools import partial

import jax
import jax.numpy as jnp
from jax import lax
from jax.experimental import pallas as pl
from jax.experimental.pallas import tpu as pltpu
from jax.sharding import PartitionSpec as P

D = 1024
HD = 64
SEQ = 577
PAD = 592
EPSILON = 1e-06
BF = jnp.bfloat16
F32 = jnp.float32
LOG2E = 1.4426950408889634
ROOT_HALF = 0.7071067811865476
DENSITY = 0.3989422804014327
KEYS_A = 512
EXPAND_CUT = 1024
LIGHT = 128
PIECES = (slice(0, 304), slice(304, PAD))
QUERY_CUTS = (0, 208, 400, PAD)
MEBI = 1 << 20


def dot_nn(left, right):
    return lax.dot_general(left, right, (((1,), (0,)), ((), ())), preferred_element_type=F32)


def dot_nt(left, right):
    return lax.dot_general(left, right, (((1,), (1,)), ((), ())), preferred_element_type=F32)


def dot_tn(left, right):
    return lax.dot_general(left, right, (((0,), (0,)), ((), ())), preferred_element_type=F32)


def whole(array):
    return pl.BlockSpec(array.shape, lambda *_: (0,) * array.ndim, pipeline_mode=pl.Buffered(1))


def by_image(width):
    return pl.BlockSpec((PAD, width), lambda i: (i, 0))


def call(kernel, name, grid, operands, outputs, macs, after=(), into=None, weight=1):
    if into is not None:
        after = (into, *after)
    size = sum(a.size * a.dtype.itemsize for _, a in operands)
    size += sum(jnp.dtype(t).itemsize * s[0] * s[1] for _, s, t in outputs)
    used = len(operands)

    def body_of(*refs):
        kernel(*refs[:used], *refs[used + len(after) :])

    return pl.pallas_call(
        body_of,
        grid=grid,
        in_specs=[s for s, _ in operands] + [pl.BlockSpec(memory_space=pl.ANY)] * len(after),
        out_specs=[s for s, _, _ in outputs],
        out_shape=[jax.ShapeDtypeStruct(s, t) for _, s, t in outputs],
        compiler_params=pltpu.CompilerParams(vmem_limit_bytes=60 * MEBI),
        cost_estimate=pl.CostEstimate(flops=2 * macs // weight, bytes_accessed=size // weight, transcendentals=0),
        input_output_aliases={} if into is None else {used: 0},
        name=name,
    )(*[a for _, a in operands], *after)


def shift(values, axis, step):
    size = lax.axis_size(axis)
    return lax.ppermute(values, axis, [(i, (i + step) % size) for i in range(size)])


def gather_blocks(block, axis):
    return [block] + [shift(block, axis, -s) for s in range(1, lax.axis_size(axis))]


def gather_weight(weight):
    return [gather_blocks(block, "col") for block in gather_blocks(weight, "row")]


def fetch_shares(weights):
    place = lax.axis_index("dp")
    depths = [w.shape[0] // lax.axis_size("dp") for w in weights]
    shares = [lax.dynamic_slice_in_dim(w, place * d, d) for w, d in zip(weights, depths)]
    widths = [w.shape[1] for w in weights]
    fetched = gather_blocks(jnp.concatenate(shares, 1), "row")[1:]
    ends = [sum(widths[: n + 1]) for n in range(len(widths))]
    return [[f[:, end - w : end] for f in fetched] for end, w in zip(ends, widths)]


def gather_shares(weight, shares, after=None):
    blocks = [lax.all_gather(s, "dp", axis=0, tiled=True) for s in shares]
    blocks = [weight] + (blocks if after is None else hold(blocks, after))
    return [gather_blocks(block, "col") for block in blocks]


def hold(values, after):
    return lax.optimization_barrier((values, after))[0]


def swap(values, axis, step):
    return lax.ppermute(values, axis, [(i, i ^ step) for i in range(lax.axis_size(axis))])


def steps_of(axis):
    steps = [1]
    while steps[-1] * 2 < lax.axis_size(axis):
        steps.append(steps[-1] * 2)
    return steps


def sum_all(values, axis):
    for step in steps_of(axis):
        values = values + swap(values, axis, step)
    return values


def halve(values, axis, step):
    half = values.shape[0] // 2
    bit = lax.axis_index(axis) // step % 2
    keep = lax.dynamic_slice_in_dim(values, bit * half, half)
    give = lax.dynamic_slice_in_dim(values, (1 - bit) * half, half)
    return (keep.astype(F32) + swap(give, axis, step).astype(F32)).astype(BF)


def join(values, axis, step):
    other = swap(values, axis, step)
    low = lax.axis_index(axis) // step % 2 == 0
    return jnp.where(low, jnp.concatenate([values, other]), jnp.concatenate([other, values]))


def sum_shares(values, axis):
    for step in steps_of(axis):
        values = halve(values, axis, step)
    for step in reversed(steps_of(axis)):
        values = join(values, axis, step)
    return values


def pack_kernel(masked, place_ref, valid_ref, x_ref, *refs):
    o_refs = refs[-lax.axis_size("row") :]
    images = o_refs[0].shape[0] // PAD
    for place in range(len(o_refs)):

        @pl.when(place_ref[0] == place)
        def _(place=place):
            for s, o_ref in enumerate(o_refs):
                at = (place - s) % len(o_refs) * images
                for i in range(images):
                    rows = x_ref[(at + i) * SEQ : (at + i + 1) * SEQ]
                    if masked:
                        rows = (rows.astype(F32) * valid_ref[at + i].astype(F32)).astype(rows.dtype)
                    o_ref[i * PAD : i * PAD + SEQ] = rows
                    rest = (PAD - SEQ, x_ref.shape[1])
                    o_ref[i * PAD + SEQ : (i + 1) * PAD] = jnp.zeros(rest, x_ref.dtype)


def pack_rows(values, place, valid, masked, after=()):
    rows, width = values.shape
    parts = lax.axis_size("row")
    vmem, smem = pl.BlockSpec(memory_space=pltpu.VMEM), pl.BlockSpec(memory_space=pltpu.SMEM)
    part = jax.ShapeDtypeStruct((rows // SEQ // parts * PAD, width), values.dtype)
    return pl.pallas_call(
        partial(pack_kernel, masked),
        in_specs=[smem, smem, vmem] + [pl.BlockSpec(memory_space=pl.ANY)] * len(after),
        out_specs=[vmem] * parts,
        out_shape=[part] * parts,
        compiler_params=pltpu.CompilerParams(vmem_limit_bytes=60 * MEBI),
        cost_estimate=pl.CostEstimate(flops=0, bytes_accessed=values.size // 8, transcendentals=0),
        name="pack_rows",
    )(place.reshape(1), valid, values, *after)


def unpack_kernel(counts, place_ref, *refs):
    o_ref = refs[-1]
    for place in range(len(counts)):

        @pl.when(place_ref[0] == place)
        def _(place=place):
            n = 0
            for s, some in enumerate(counts):
                at = (place - s) % len(counts) * sum(some)
                for count in some:
                    for i in range(count):
                        rows = refs[n][i * PAD : i * PAD + SEQ].astype(o_ref.dtype)
                        o_ref[at * SEQ : (at + 1) * SEQ] = rows
                        at += 1
                    n += 1


def unpack_rows(parts, place, dtype):
    counts = tuple(tuple(a.shape[0] // PAD for a in some) for some in parts)
    arrays = [a for some in parts for a in some]
    vmem = pl.BlockSpec(memory_space=pltpu.VMEM)
    return pl.pallas_call(
        partial(unpack_kernel, counts),
        in_specs=[pl.BlockSpec(memory_space=pltpu.SMEM)] + [vmem] * len(arrays),
        out_specs=vmem,
        out_shape=jax.ShapeDtypeStruct(
            (sum(map(sum, counts)) * SEQ, arrays[0].shape[1]), dtype
        ),
        compiler_params=pltpu.CompilerParams(vmem_limit_bytes=60 * MEBI),
        cost_estimate=pl.CostEstimate(
            flops=0, bytes_accessed=arrays[0].size // 8, transcendentals=0
        ),
        name="unpack_rows",
    )(place.reshape(1), *arrays)


def row_mean(blocks):
    return sum(jnp.sum(b, 1, keepdims=True) for b in blocks) / (len(blocks) * blocks[0].shape[1])


def normalize(blocks):
    center = row_mean(blocks)
    inverse = lax.rsqrt(row_mean([b * b for b in blocks]) - center * center + EPSILON)
    return [(b - center) * inverse for b in blocks], inverse


def norm_back(upstream, scaled, inverse, gains):
    grads = [u * g for u, g in zip(upstream, gains)]
    plain = row_mean(grads)
    cross = row_mean([g * x for g, x in zip(grads, scaled)])
    return [inverse * (g - plain - x * cross) for g, x in zip(grads, scaled)]


def cut(values, width):
    return [values[:, at : at + width] for at in range(0, values.shape[1], width)]


def add_rows(ref, values, at=0):
    ref[:, at : at + values.shape[1]] += jnp.sum(values, 0, keepdims=True)


def grid_of(refs, shape):
    outer, inner = shape
    return [refs[i * inner : (i + 1) * inner] for i in range(outer)]


def project_kernel(shape, gain_ref, shift_ref, bias_ref, *refs):
    rows, cols = shape
    x_refs, weights = refs[:rows], grid_of(refs[rows : rows + rows * cols], shape)
    normed_ref, packed_ref = refs[rows + rows * cols :]
    width, block = weights[0][0].shape
    gains, shifts = cut(gain_ref[...], width), cut(shift_ref[...], width)
    for some in PIECES:
        scaled, _ = normalize([x[some, :].astype(F32) for x in x_refs])
        normed = [(x * g + b).astype(BF) for x, g, b in zip(scaled, gains, shifts)]
        for i, n in enumerate(normed):
            normed_ref[some, i * width : (i + 1) * width] = n
        for j in range(cols):
            total = sum(dot_nn(n, weights[i][j][...]) for i, n in enumerate(normed))
            where = slice(j * block, (j + 1) * block)
            packed_ref[some, where] = (total + bias_ref[:, where]).astype(BF)


def swap_halves(values):
    return jnp.concatenate([values[:, HD:], values[:, :HD]], 1)


def attend_kernel(p_ref, o_ref):
    first, second, third = p_ref[:, :128], p_ref[:, 128:256], p_ref[:, 256:]
    low = lax.broadcasted_iota(jnp.int32, (1, 128), 1) < HD
    zero, one = jnp.zeros((), BF), jnp.ones((), BF)
    queries = (jnp.where(low, first, zero), jnp.where(low, swap_halves(second), zero))
    keys = (swap_halves(first), third)
    values = (jnp.where(low, second, one), jnp.where(low, one, third))
    scale = HD**-0.5 * LOG2E
    keep = lax.broadcasted_iota(jnp.int32, (1, PAD - KEYS_A), 1) < SEQ - KEYS_A
    units = [(slice(*cut), h) for cut in zip(QUERY_CUTS, QUERY_CUTS[1:]) for h in range(2)]
    scores = [
        (dot_nt(queries[h][some], keys[h][:KEYS_A]), dot_nt(queries[h][some], keys[h][KEYS_A:]))
        for some, h in units
    ]
    weights = []
    for sa, sb in scores:
        sb = jnp.where(keep, sb, -1e30)
        top = jnp.maximum(jnp.max(sa, 1, keepdims=True), jnp.max(sb, 1, keepdims=True)) * scale
        weights.append([jnp.exp2(v * scale - top).astype(BF) for v in (sa, sb)])
    outs = [
        dot_nn(pa, values[h][:KEYS_A]) + dot_nn(pb, values[h][KEYS_A:])
        for (_, h), (pa, pb) in zip(units, weights)
    ]
    for n in range(0, len(units), 2):
        mixed, totals = jnp.where(low, *outs[n : n + 2]), jnp.where(low, *outs[n : n + 2][::-1])
        o_ref[units[n][0], :] = (mixed / swap_halves(totals)).astype(BF)


def attend(packed, first, some, into, after):
    tokens, width = packed.shape
    pairs = width // (6 * HD)
    return call(
        attend_kernel,
        "attend",
        (some, tokens // PAD),
        [(pl.BlockSpec((PAD, 6 * HD), lambda h, i: (i, first + h)), packed)],
        [
            (
                pl.BlockSpec((PAD, 2 * HD), lambda h, i: (i, first + h)),
                (tokens, pairs * 2 * HD),
                BF,
            )
        ],
        tokens * PAD * some * 2 * HD * 5,
        after,
        into,
    )[0]


def attend_back_kernel(p_ref, g_ref, o_ref):
    first, second, third = p_ref[:, :128], p_ref[:, 128:256], p_ref[:, 256:]
    grad = g_ref[...]
    low = lax.broadcasted_iota(jnp.int32, (1, 128), 1) < HD
    zero = jnp.zeros((), BF)
    turned = [swap_halves(v) for v in (first, second, third)]
    queries = (jnp.where(low, first, zero), jnp.where(low, turned[1], zero))
    keys, values = (turned[0], third), (second, third)
    grads = (jnp.where(low, grad, zero), jnp.where(low, zero, grad))
    query_right = (turned[0], turned[1])
    key_right = (turned[0], turned[2])
    scale = HD**-0.5
    edge = PAD - 16
    keep = lax.broadcasted_iota(jnp.int32, (PAD - edge, 1), 0) < SEQ - edge
    units = [(slice(at, min(PAD, at + 256)), h) for at in range(0, PAD, 256) for h in range(2)]
    products = [
        (dot_nt(keys[h], queries[h][some]), dot_nt(values[h], grads[h][some])) for some, h in units
    ]
    lows = []
    for scores, weight_grad in products:
        sa, sb = scores[:edge], jnp.where(keep, scores[edge:], -1e30)
        top = jnp.maximum(jnp.max(sa, 0, keepdims=True), jnp.max(sb, 0, keepdims=True))
        top = top * (scale * LOG2E)
        weights = jnp.concatenate([jnp.exp2(s * (scale * LOG2E) - top) for s in (sa, sb)], 0)
        share = 1.0 / jnp.sum(weights, 0, keepdims=True)
        product = weights * weight_grad
        row_dot = jnp.sum(product, 0, keepdims=True) * share
        score_low = (product - weights * row_dot) * share
        lows.append(((weights * share).astype(BF), score_low.astype(BF)))
    value_grad, key_grad, query_grad = [0.0, 0.0], [0.0, 0.0], [[], []]
    for (some, h), (weights, score_low) in zip(units, lows):
        value_grad[h] += dot_nn(weights, grad[some])
        key_grad[h] += dot_nn(score_low, query_right[h][some])
        query_grad[h].append(dot_tn(key_right[h], score_low).T)
    query_grad = [jnp.concatenate(q, 0) for q in query_grad]
    o_ref[:, :128] = (jnp.where(low, query_grad[0], key_grad[0]) * scale).astype(BF)
    o_ref[:, 128:256] = jnp.where(low, value_grad[0], query_grad[1] * scale).astype(BF)
    o_ref[:, 256:] = jnp.where(low, key_grad[1] * scale, value_grad[1]).astype(BF)


def attend_back(packed, grad, cols, pair, slot, slots, into, after):
    tokens, width = packed.shape
    block = width // (6 * HD) // cols
    return call(
        attend_back_kernel,
        "attend_back",
        (cols, tokens // PAD),
        [
            (pl.BlockSpec((PAD, 6 * HD), lambda j, i: (i, j * block + pair)), packed),
            (pl.BlockSpec((PAD, 2 * HD), lambda j, i: (i, j * block + pair)), grad),
        ],
        [
            (
                pl.BlockSpec((PAD, 6 * HD), lambda j, i: (i, j * slots + slot)),
                (tokens, cols * slots * 6 * HD),
                BF,
            )
        ],
        tokens * PAD * cols * 2 * HD * 12,
        after,
        into,
        LIGHT,
    )[0]


def output_kernel(shape, bias_ref, gain_ref, shift_ref, mixed_ref, *refs):
    rows, cols = shape
    x_refs, weights = refs[:rows], grid_of(refs[rows : rows + rows * cols], shape)
    middle_ref, normed_ref = refs[rows + rows * cols :]
    block, width = weights[0][0].shape
    spans = [slice(i * width, (i + 1) * width) for i in range(rows)]
    totals = []
    for some in PIECES:
        mixed = cut(mixed_ref[some, :], block)
        totals.append(
            [
                sum(dot_nn(m, weights[i][j][...]) for j, m in enumerate(mixed))
                for i in range(rows)
            ]
        )
    for some, total in zip(PIECES, totals):
        middle = []
        for i, where in enumerate(spans):
            middle.append(x_refs[i][some, :].astype(F32) + total[i] + bias_ref[:, where])
            middle_ref[some, where] = middle[-1]
        scaled, _ = normalize(middle)
        for x, where in zip(scaled, spans):
            normed = x * gain_ref[:, where] + shift_ref[:, where]
            normed_ref[some, where] = normed.astype(BF)


def expand_kernel(shape, bias_ref, normed_ref, *refs):
    rows, cols = shape
    weights = grid_of(refs[: rows * cols], shape)
    hidden_ref, slope_ref = refs[rows * cols :]
    depth, block = weights[0][0].shape
    cuts = [
        (some, j, at)
        for some in PIECES
        for j in range(cols)
        for at in range(0, block, min(block, EXPAND_CUT))
    ]
    normed = {some.start: cut(normed_ref[some, :], depth) for some in PIECES}
    wide = min(block, EXPAND_CUT)
    totals = [
        sum(
            dot_nn(n, weights[i][j][:, at : at + wide])
            for i, n in enumerate(normed[some.start])
        )
        for some, j, at in cuts
    ]
    for (some, j, at), total in zip(cuts, totals):
        where = slice(j * block + at, j * block + at + wide)
        before = total + bias_ref[:, where]
        below = 0.5 + 0.5 * lax.erf(before * ROOT_HALF)
        hidden_ref[some, where] = (before * below).astype(BF)
        density = jnp.exp2(before * before * (-0.5 * LOG2E)) * DENSITY
        slope_ref[some, where] = (below + before * density).astype(BF)


def reduce_kernel(shape, valid_ref, bias_ref, hidden_ref, middle_ref, *refs):
    rows, cols = shape
    weights, o_refs = grid_of(refs[: rows * cols], shape), refs[rows * cols :]
    block, width = weights[0][0].shape
    valid = valid_ref[pl.program_id(0)].astype(F32)
    for i in range(rows):
        total = sum(
            dot_nn(hidden_ref[:, j * block : (j + 1) * block], weights[i][j][...])
            for j in range(cols)
        )
        where = slice(i * width, (i + 1) * width)
        o_refs[i][...] = ((middle_ref[:, where] + total + bias_ref[:, where]) * valid).astype(BF)


def reduce_back_kernel(shape, slope_ref, *refs):
    rows, cols = shape
    g_refs, weights = refs[:rows], grid_of(refs[rows : rows + rows * cols], shape)
    before_ref, reduce_bias_ref, expand_bias_ref = refs[rows + rows * cols :]

    @pl.when(pl.program_id(0) == 0)
    def _():
        reduce_bias_ref[...] = jnp.zeros_like(reduce_bias_ref)
        expand_bias_ref[...] = jnp.zeros_like(expand_bias_ref)

    block, width = weights[0][0].shape
    lows = [g[...] for g in g_refs]
    for i, low in enumerate(lows):
        add_rows(reduce_bias_ref, low.astype(F32), i * width)
    for j in range(cols):
        total = sum(dot_nt(low, weights[i][j][...]) for i, low in enumerate(lows))
        where = slice(j * block, (j + 1) * block)
        total = total * slope_ref[:, where].astype(F32)
        add_rows(expand_bias_ref, total, j * block)
        before_ref[:, where] = total.astype(BF)


def expand_back_kernel(shape, gain_ref, before_ref, middle_ref, *refs):
    rows, cols = shape
    g_refs, refs = refs[:rows], refs[rows:]
    count = rows * cols
    expand, output = grid_of(refs[:count], shape), grid_of(refs[count : 2 * count], shape)
    refs = refs[2 * count :]
    middle_grad_ref, mixed_low_ref, gain_grad, shift_grad, bias_grad = refs[:5]
    low_refs = refs[5:]

    @pl.when(pl.program_id(0) == 0)
    def _():
        for ref in (gain_grad, shift_grad, bias_grad):
            ref[...] = jnp.zeros_like(ref)

    width, block = expand[0][0].shape
    spans = [slice(i * width, (i + 1) * width) for i in range(rows)]
    heads = output[0][0].shape[0]
    upstreams = [
        [
            sum(
                dot_nt(before_ref[some, j * block : (j + 1) * block], expand[i][j][...])
                for j in range(cols)
            )
            for i in range(rows)
        ]
        for some in PIECES
    ]
    for some, upstream in zip(PIECES, upstreams):
        scaled, inverse = normalize(cut(middle_ref[some, :], width))
        parts = norm_back(upstream, scaled, inverse, cut(gain_ref[...], width))
        lows = []
        for i, part in enumerate(parts):
            add_rows(gain_grad, upstream[i] * scaled[i], i * width)
            add_rows(shift_grad, upstream[i], i * width)
            grad = g_refs[i][some, :].astype(F32) + part
            add_rows(bias_grad, grad, i * width)
            middle_grad_ref[some, spans[i]] = grad
            lows.append(grad.astype(BF))
            low_refs[i][some, :] = lows[-1]
        for j in range(cols):
            total = sum(dot_nt(low, output[i][j][...]) for i, low in enumerate(lows))
            mixed_low_ref[some, j * heads : (j + 1) * heads] = total.astype(BF)


def project_back_kernel(shape, parts, gain_ref, middle_ref, *refs):
    rows, cols = shape
    packed, refs = refs[:parts], refs[parts:]
    x_refs, weights = refs[:rows], grid_of(refs[rows : rows + rows * cols], shape)
    refs = refs[rows + rows * cols :]
    o_refs, (gain_grad, shift_grad), bias_grads = refs[:rows], refs[rows : rows + 2], refs[rows + 2 :]

    @pl.when(pl.program_id(0) == 0)
    def _():
        for ref in refs[rows:]:
            ref[...] = jnp.zeros_like(ref)

    width = weights[0][0].shape[0]
    for p in range(parts):
        add_rows(bias_grads[p], packed[p][...].astype(F32))
    upstreams = []
    for piece in PIECES:
        upstream = [0.0] * rows
        at = 0
        for p in range(parts):
            some = packed[p].shape[1] // cols
            for j in range(cols):
                grad = packed[p][piece, j * some : (j + 1) * some]
                for i in range(rows):
                    upstream[i] += dot_nt(grad, weights[i][j][:, at : at + some])
            at += some
        upstreams.append(upstream)
    for piece, upstream in zip(PIECES, upstreams):
        scaled, inverse = normalize([x[piece, :].astype(F32) for x in x_refs])
        grads = norm_back(upstream, scaled, inverse, cut(gain_ref[...], width))
        for i, grad in enumerate(grads):
            add_rows(gain_grad, upstream[i] * scaled[i], i * width)
            add_rows(shift_grad, upstream[i], i * width)
            total = middle_ref[piece, i * width : (i + 1) * width] + grad
            o_refs[i][piece, :] = total.astype(o_refs[i].dtype)


def outer_kernel(rights, received, whole_width, a_ref, *refs):
    b_refs, refs = refs[:rights], refs[rights:]
    received, o_refs = refs[:received], refs[received:]
    height, width = o_refs[0].shape
    left = a_ref[...]
    at = 0
    for b_ref in b_refs:
        total = dot_tn(left, b_ref[...])
        where = slice(at, at + total.shape[1])
        for ref in received:
            total += ref[:, where].astype(F32)
        total = total.astype(BF)
        if width < whole_width:
            o_refs[at // width][...] = total
        else:
            for n, o_ref in enumerate(o_refs):
                o_ref[:, where] = total[n * height : (n + 1) * height]
        at = where.stop


def outer(left, rights, left_part, right_part, name, after, received=(), splits=(1, 1)):
    tokens = left.shape[0]
    (li, lw), (ri, rw) = left_part, right_part
    bl, br = min(lw, 1024), 1024 if rw % 1024 == 0 else rw
    down, across = splits
    tile = pl.BlockSpec((bl, br), lambda i, j: (i, j))
    part = pl.BlockSpec((bl // down, br // across), lambda i, j: (i, j))
    spec = pl.BlockSpec((tokens, br // len(rights)), lambda i, j: (0, ri * (rw // br) + j))
    return call(
        partial(outer_kernel, len(rights), len(received), br),
        name,
        (lw // bl, rw // br),
        [(pl.BlockSpec((tokens, bl), lambda i, j: (0, li * (lw // bl) + i)), left)]
        + [(spec, right) for right in rights]
        + [(tile, r) for r in received],
        [(part, (lw // down, rw // across), BF)] * (down * across),
        tokens * lw * rw,
        after,
        weight=1 if name in ("reduce_outer", "expand_outer") else LIGHT,
    )


def body(
    block_input,
    image_valid,
    first_gain,
    first_shift,
    attend_weight,
    attend_bias,
    output_weight,
    output_bias,
    second_gain,
    second_shift,
    expand_weight,
    expand_bias,
    reduce_weight,
    reduce_bias,
    output_grad,
):
    rows, cols = lax.axis_size("row"), lax.axis_size("col")
    row_index, col_index = lax.axis_index("row"), lax.axis_index("col")
    local_rows, width = block_input.shape
    local_images = local_rows // SEQ
    images = local_images // rows
    tokens = images * PAD
    hidden_width = expand_weight.shape[1] * cols
    shape = (rows, cols)
    step = (images,)

    local_valid = lax.dynamic_slice_in_dim(image_valid, col_index * local_images, local_images)

    def to_tokens(values, masked, after=()):
        parts = pack_rows(values, row_index, local_valid, masked, after)
        return [shift(part, "row", -s) if s else part for s, part in enumerate(parts)]

    def sent(parts):
        return [shift(a, "row", s) if s else a for s, a in enumerate(parts)]

    features = jnp.stack(
        [first_gain, first_shift, output_bias, second_gain, second_shift, reduce_bias]
    )
    features = jnp.concatenate(gather_blocks(features, "row"), 1).astype(F32)
    first_gain, first_shift, output_bias, second_gain, second_shift, reduce_bias = jnp.split(
        features, 6, 0
    )
    biases = jnp.stack(gather_blocks(jnp.concatenate([attend_bias, expand_bias]), "col"))
    biases = biases.astype(F32)
    pairs = biases[:, : attend_bias.shape[0]].reshape(-1, 2, HD)
    attend_bias = jnp.stack([pairs[:, 0], jnp.zeros_like(pairs[:, 0]), pairs[:, 1]], 1)
    attend_bias = attend_bias.reshape(1, 3 * D)
    expand_bias = biases[:, -expand_bias.shape[0] :].reshape(1, -1)
    valid = lax.dynamic_slice_in_dim(
        image_valid, col_index * local_images + row_index * images, images
    )

    inputs = to_tokens(block_input, False)
    attend_shares, expand_shares = hold(fetch_shares([attend_weight, expand_weight]), inputs[0])
    attend_blocks = gather_shares(attend_weight, attend_shares)
    output_rows = gather_blocks(hold(output_weight, inputs), "row")

    def flat(blocks):
        return [(whole(b), b) for some in blocks for b in some]

    def row_blocks(arrays):
        return [(by_image(width), a) for a in arrays]

    def full(array):
        return (whole(array), array)

    def image(array):
        return (by_image(array.shape[1]), array)

    def out(columns, dtype):
        return (by_image(columns), (tokens, columns), dtype)

    def total(columns):
        return (pl.BlockSpec((1, columns), lambda i: (0, 0)), (1, columns), F32)

    scalars = (pl.BlockSpec(memory_space=pltpu.SMEM), valid)

    first_normed, packed = call(
        partial(project_kernel, shape),
        "project",
        step,
        [full(first_gain), full(first_shift), full(attend_bias)]
        + row_blocks(inputs)
        + flat(attend_blocks),
        [out(D, BF), out(3 * D, BF)],
        tokens * 3 * D * D,
    )
    grads = to_tokens(output_grad, True, (packed,))
    (reduce_shares,) = fetch_shares([hold(reduce_weight, packed)])
    pairs = packed.shape[1] // (6 * HD)
    mixed = attend(packed, 0, pairs // 4, None, (*expand_shares, *reduce_shares, grads[0]))
    expand_blocks = gather_shares(expand_weight, expand_shares, mixed)
    reduce_shares = hold(reduce_shares, mixed)
    mixed = attend(packed, pairs // 4, pairs - pairs // 4, mixed, reduce_shares)
    output_blocks = [gather_blocks(block, "col") for block in hold(output_rows, mixed)]
    middle, second_normed = call(
        partial(output_kernel, shape),
        "output",
        step,
        [full(output_bias), full(second_gain), full(second_shift), image(mixed)]
        + row_blocks(inputs)
        + flat(output_blocks),
        [out(D, F32), out(D, BF)],
        tokens * D * D,
    )
    reduce_blocks = gather_shares(reduce_weight, reduce_shares, second_normed)
    hidden, slope = call(
        partial(expand_kernel, shape),
        "expand",
        step,
        [full(expand_bias), image(second_normed)] + flat(expand_blocks),
        [out(hidden_width, BF), out(hidden_width, BF)],
        tokens * D * hidden_width,
        (*reduce_blocks[0][1:], *reduce_blocks[-1][:1]),
    )
    def add_parts(parts, axis, after=None):
        held = parts[0].astype(F32)
        others = [shift(part, axis, s) for s, part in enumerate(parts) if s]
        for other in others if after is None else hold(others, after):
            held = held + other.astype(F32)
        return held

    def places(left, rights, over_left, j):
        lw, rw = left.shape[1], sum(r.shape[1] for r in rights)
        return ((j, lw // cols), (0, rw)) if over_left else ((0, lw), (j, rw // cols))

    def outer_others(left, rights, over_left, name, after=()):
        received = []
        for j in range(1, cols):
            (block,) = outer(left, rights, *places(left, rights, over_left, j), name, after)
            received.append(shift(block, "col", j))
            after = (block,)
        return received, after

    def outer_own(left, rights, over_left, name, others, after=()):
        received, order = others
        splits = (1, rows) if over_left else (rows, 1)
        where = places(left, rights, over_left, 0)
        return outer(left, rights, *where, name, (*order, *after), received, splits)

    def share_of(held, after=None):
        received = [shift(part, "row", s) for s, part in enumerate(held) if s]
        total = held[0].astype(F32)
        for part in received if after is None else hold(received, after):
            total = total + part.astype(F32)
        return total.astype(BF), received

    reduce_others = outer_others(hidden, grads, True, "reduce_outer", reduce_blocks[-1][:1])
    before_low, reduce_bias_grad, expand_bias_grad = call(
        partial(reduce_back_kernel, shape),
        "reduce_back",
        step,
        [image(slope)] + row_blocks(grads) + flat(reduce_blocks),
        [out(hidden_width, BF), total(D), total(hidden_width)],
        tokens * D * hidden_width,
        reduce_others[1],
        weight=LIGHT,
    )
    reduce_held = outer_own(hidden, grads, True, "reduce_outer", reduce_others, (before_low,))
    reduce_share, reduce_received = share_of(reduce_held)
    expand_others = outer_others(
        second_normed, [before_low], False, "expand_outer", reduce_held[:1]
    )
    middle_grad, mixed_low, second_gain_grad, second_shift_grad, output_bias_grad, *middle_lows = call(
        partial(expand_back_kernel, shape),
        "expand_back",
        step,
        [full(second_gain), image(before_low), image(middle)]
        + row_blocks(grads)
        + flat(expand_blocks)
        + flat(output_blocks),
        [out(D, F32), out(D, BF), total(D), total(D), total(D)] + [out(width, BF)] * rows,
        tokens * D * (hidden_width + D),
        expand_others[1],
        weight=LIGHT,
    )
    expand_held = outer_own(
        second_normed, [before_low], False, "expand_outer", expand_others, (middle_grad, *reduce_received)
    )
    output_others = outer_others(mixed, middle_lows, True, "output_outer", expand_held[:1])
    output_held = outer_own(mixed, middle_lows, True, "output_outer", output_others)

    reduce_weight_grad = lax.psum(reduce_share, "dp")
    expand_share, expand_received = share_of(expand_held)
    output_share, output_received = share_of(output_held)
    expand_weight_grad, output_weight_grad = lax.psum(
        hold((expand_share, output_share), reduce_weight_grad), "dp"
    )
    pairs = 3 * D // (6 * HD) // cols
    counts = [pairs - 2, 1, 1] if pairs > 2 else [pairs]
    packed_lows, held, shares, halved, arrived, pair = [], [], [], [], (), 0
    ready = output_held[:1]
    for g, count in enumerate(counts):
        packed_low = None
        for slot in range(count):
            packed_low = attend_back(
                packed, mixed_low, cols, pair, slot, count, packed_low, ready
            )
            ready = []
            if pair == 0:
                results = call(
                    partial(reduce_kernel, shape),
                    "reduce",
                    step,
                    [scalars, full(reduce_bias), image(hidden), image(middle)] + flat(reduce_blocks),
                    [out(width, BF)] * rows,
                    tokens * D * hidden_width,
                    (packed_low,),
                    weight=LIGHT,
                )
                block_output = unpack_rows([[part] for part in sent(results)], row_index, BF)
                ready = [results[0], *expand_received, *output_received]
            pair += 1
        packed_lows.append(packed_low)
        last, own_last = (reduce_weight_grad,) if g == 0 else (), ()
        if g == 2:
            last, own_last = (halved[1],), (halved[2],)
        others = outer_others(first_normed, [packed_low], False, "project_outer", last)
        held.append(outer_own(first_normed, [packed_low], False, "project_outer", others, own_last))
        ready = (held[g][0],)
        if g == 0:
            shares.append(share_of(held[0])[0])
            halved.append(shares[0])
            for hop in steps_of("dp"):
                halved.append(halve(halved[-1], "dp", hop))
            ready += (block_output,)
        elif g == 1:
            shares.append(share_of(held[1])[0])
            ready += (shares[0],)
        else:
            ready += (halved[3], expand_weight_grad)
    joined = halved[-1:]
    for hop in reversed(steps_of("dp")):
        joined.append(join(joined[-1], "dp", hop))

    halves = 2 if images % 2 == 0 else 1
    some = images // halves
    input_grads, sums = [], 0.0
    for half in range(halves):

        def later(array):
            place = half * some
            spec = pl.BlockSpec((PAD, array.shape[1]), lambda i: (i + place, 0))
            return (spec, array)

        def here(dtype):
            return (by_image(width), (some * PAD, width), dtype)

        results = call(
            partial(project_back_kernel, shape, len(counts)),
            "project_back",
            (some,),
            [full(first_gain), later(middle_grad)]
            + [later(p) for p in packed_lows]
            + [later(x) for x in inputs]
            + flat(attend_blocks),
            [here(F32)]
            + [here(BF)] * (rows - 1)
            + [total(D), total(D)]
            + [total(p.shape[1]) for p in packed_lows],
            some * PAD * 3 * D * D,
            ready,
            weight=LIGHT,
        )
        input_grads.append(sent(results[:rows]))
        if half == 0 and len(counts) > 1:
            share, arrived = share_of(held[-1], results[0])
            shares.append(share)
        ready = (results[0], *arrived, joined[1])
        packed_sums = [v.reshape(cols, -1, 3, HD) for v in results[rows + 2 :]]
        late = (*results[rows : rows + 2], jnp.concatenate(packed_sums, 1))
        sums = late if half == 0 else jax.tree.map(jnp.add, sums, late)
    input_grad = unpack_rows(list(zip(*input_grads)), row_index, F32)
    first_gain_grad, first_shift_grad, packed_sums = sums
    attend_weight_grad = joined[-1:]
    if len(shares) > 1:
        attend_weight_grad.append(sum_shares(jnp.concatenate(shares[1:], 1), "dp"))
    attend_weight_grad = jnp.concatenate(attend_weight_grad, 1)

    feature_grads = jnp.concatenate(
        [
            first_gain_grad,
            first_shift_grad,
            output_bias_grad,
            second_gain_grad,
            second_shift_grad,
            reduce_bias_grad,
        ]
    )
    attend_bias_grad = jnp.stack([packed_sums[:, :, 0], packed_sums[:, :, 2]], 2)
    attend_bias_grad = attend_bias_grad.reshape(cols, -1)
    bias_grads = jnp.concatenate([attend_bias_grad, expand_bias_grad.reshape(cols, -1)], 1)
    bias_grads = add_parts(list(bias_grads), "col")
    feature_grads = sum_all(feature_grads.reshape(-1), "col")
    small = hold(jnp.concatenate([feature_grads, bias_grads]), input_grads[0][-1])
    small = hold(sum_all(small, "dp"), input_grads[-1][-1])
    feature_grads, bias_grads = small[: 6 * D].reshape(6, D), small[6 * D :]
    feature_grads = add_parts(jnp.split(feature_grads, rows, 1), "row")
    bias_grads = sum_all(bias_grads, "row")
    split = attend_bias_grad.shape[1]
    return (
        block_output,
        input_grad,
        feature_grads[0],
        feature_grads[1],
        attend_weight_grad.astype(F32),
        bias_grads[:split],
        output_weight_grad.astype(F32),
        feature_grads[2],
        feature_grads[3],
        feature_grads[4],
        expand_weight_grad.astype(F32),
        bias_grads[split:],
        reduce_weight_grad.astype(F32),
        feature_grads[5],
    )


def solution(mesh):
    tokens = P(("dp", "col"), "row")
    by_row, by_col = P("row"), P("col")
    up, down = P("row", "col"), P("col", "row")
    params = (by_row, by_row, up, by_col, down, by_row, by_row, by_row, up, by_col, down, by_row)
    return jax.shard_map(
        body,
        mesh=mesh,
        in_specs=(tokens, P("dp")) + params + (tokens,),
        out_specs=(tokens, tokens) + params,
        check_vma=False,
    )
```

```python
from functools import partial

import jax
import jax.numpy as jnp
from jax import lax
from jax.experimental import pallas as pl
from jax.experimental.pallas import tpu as pltpu
from jax.sharding import PartitionSpec as P

D = 1024
HD = 64
SEQ = 577
PAD = 592
EPSILON = 1e-06
BF = jnp.bfloat16
F32 = jnp.float32
LOG2E = 1.4426950408889634
ROOT_HALF = 0.7071067811865476
DENSITY = 0.3989422804014327
KEYS_A = 512
EXPAND_CUT = 1024
LIGHT = 128
PIECES = (slice(0, 304), slice(304, PAD))
QUERY_CUTS = (0, 208, 400, PAD)
MEBI = 1 << 20


def dot_nn(left, right):
    return lax.dot_general(left, right, (((1,), (0,)), ((), ())), preferred_element_type=F32)


def dot_nt(left, right):
    return lax.dot_general(left, right, (((1,), (1,)), ((), ())), preferred_element_type=F32)


def dot_tn(left, right):
    return lax.dot_general(left, right, (((0,), (0,)), ((), ())), preferred_element_type=F32)


def whole(array):
    return pl.BlockSpec(array.shape, lambda *_: (0,) * array.ndim, pipeline_mode=pl.Buffered(1))


def by_image(width):
    return pl.BlockSpec((PAD, width), lambda i: (i, 0))


def call(kernel, name, grid, operands, outputs, macs, after=(), into=None, weight=1):
    if into is not None:
        after = (into, *after)
    size = sum(a.size * a.dtype.itemsize for _, a in operands)
    size += sum(jnp.dtype(t).itemsize * s[0] * s[1] for _, s, t in outputs)
    used = len(operands)

    def body_of(*refs):
        kernel(*refs[:used], *refs[used + len(after) :])

    return pl.pallas_call(
        body_of,
        grid=grid,
        in_specs=[s for s, _ in operands] + [pl.BlockSpec(memory_space=pl.ANY)] * len(after),
        out_specs=[s for s, _, _ in outputs],
        out_shape=[jax.ShapeDtypeStruct(s, t) for _, s, t in outputs],
        compiler_params=pltpu.CompilerParams(vmem_limit_bytes=60 * MEBI),
        cost_estimate=pl.CostEstimate(flops=2 * macs // weight, bytes_accessed=size // weight, transcendentals=0),
        input_output_aliases={} if into is None else {used: 0},
        name=name,
    )(*[a for _, a in operands], *after)


def shift(values, axis, step):
    size = lax.axis_size(axis)
    return lax.ppermute(values, axis, [(i, (i + step) % size) for i in range(size)])


def gather_blocks(block, axis):
    return [block] + [shift(block, axis, -s) for s in range(1, lax.axis_size(axis))]


def gather_weight(weight):
    return [gather_blocks(block, "col") for block in gather_blocks(weight, "row")]


def fetch_shares(weights):
    place = lax.axis_index("dp")
    depths = [w.shape[0] // lax.axis_size("dp") for w in weights]
    shares = [lax.dynamic_slice_in_dim(w, place * d, d) for w, d in zip(weights, depths)]
    widths = [w.shape[1] for w in weights]
    fetched = gather_blocks(jnp.concatenate(shares, 1), "row")[1:]
    ends = [sum(widths[: n + 1]) for n in range(len(widths))]
    return [[f[:, end - w : end] for f in fetched] for end, w in zip(ends, widths)]


def gather_shares(weight, shares, after=None):
    blocks = [lax.all_gather(s, "dp", axis=0, tiled=True) for s in shares]
    blocks = [weight] + (blocks if after is None else hold(blocks, after))
    return [gather_blocks(block, "col") for block in blocks]


def hold(values, after):
    return lax.optimization_barrier((values, after))[0]


def swap(values, axis, step):
    return lax.ppermute(values, axis, [(i, i ^ step) for i in range(lax.axis_size(axis))])


def steps_of(axis):
    steps = [1]
    while steps[-1] * 2 < lax.axis_size(axis):
        steps.append(steps[-1] * 2)
    return steps


def sum_all(values, axis):
    for step in steps_of(axis):
        values = values + swap(values, axis, step)
    return values


def halve(values, axis, step):
    half = values.shape[0] // 2
    bit = lax.axis_index(axis) // step % 2
    keep = lax.dynamic_slice_in_dim(values, bit * half, half)
    give = lax.dynamic_slice_in_dim(values, (1 - bit) * half, half)
    return (keep.astype(F32) + swap(give, axis, step).astype(F32)).astype(BF)


def join(values, axis, step):
    other = swap(values, axis, step)
    low = lax.axis_index(axis) // step % 2 == 0
    return jnp.where(low, jnp.concatenate([values, other]), jnp.concatenate([other, values]))


def sum_shares(values, axis):
    for step in steps_of(axis):
        values = halve(values, axis, step)
    for step in reversed(steps_of(axis)):
        values = join(values, axis, step)
    return values


def pack_kernel(masked, place_ref, valid_ref, x_ref, *refs):
    o_refs = refs[-lax.axis_size("row") :]
    images = o_refs[0].shape[0] // PAD
    for place in range(len(o_refs)):

        @pl.when(place_ref[0] == place)
        def _(place=place):
            for s, o_ref in enumerate(o_refs):
                at = (place - s) % len(o_refs) * images
                for i in range(images):
                    rows = x_ref[(at + i) * SEQ : (at + i + 1) * SEQ]
                    if masked:
                        rows = (rows.astype(F32) * valid_ref[at + i].astype(F32)).astype(rows.dtype)
                    o_ref[i * PAD : i * PAD + SEQ] = rows
                    rest = (PAD - SEQ, x_ref.shape[1])
                    o_ref[i * PAD + SEQ : (i + 1) * PAD] = jnp.zeros(rest, x_ref.dtype)


def pack_rows(values, place, valid, masked, after=()):
    rows, width = values.shape
    parts = lax.axis_size("row")
    vmem, smem = pl.BlockSpec(memory_space=pltpu.VMEM), pl.BlockSpec(memory_space=pltpu.SMEM)
    part = jax.ShapeDtypeStruct((rows // SEQ // parts * PAD, width), values.dtype)
    return pl.pallas_call(
        partial(pack_kernel, masked),
        in_specs=[smem, smem, vmem] + [pl.BlockSpec(memory_space=pl.ANY)] * len(after),
        out_specs=[vmem] * parts,
        out_shape=[part] * parts,
        compiler_params=pltpu.CompilerParams(vmem_limit_bytes=60 * MEBI),
        cost_estimate=pl.CostEstimate(flops=0, bytes_accessed=values.size // 8, transcendentals=0),
        name="pack_rows",
    )(place.reshape(1), valid, values, *after)


def unpack_kernel(counts, place_ref, *refs):
    o_ref = refs[-1]
    for place in range(len(counts)):

        @pl.when(place_ref[0] == place)
        def _(place=place):
            n = 0
            for s, some in enumerate(counts):
                at = (place - s) % len(counts) * sum(some)
                for count in some:
                    for i in range(count):
                        rows = refs[n][i * PAD : i * PAD + SEQ].astype(o_ref.dtype)
                        o_ref[at * SEQ : (at + 1) * SEQ] = rows
                        at += 1
                    n += 1


def unpack_rows(parts, place, dtype):
    counts = tuple(tuple(a.shape[0] // PAD for a in some) for some in parts)
    arrays = [a for some in parts for a in some]
    vmem = pl.BlockSpec(memory_space=pltpu.VMEM)
    return pl.pallas_call(
        partial(unpack_kernel, counts),
        in_specs=[pl.BlockSpec(memory_space=pltpu.SMEM)] + [vmem] * len(arrays),
        out_specs=vmem,
        out_shape=jax.ShapeDtypeStruct(
            (sum(map(sum, counts)) * SEQ, arrays[0].shape[1]), dtype
        ),
        compiler_params=pltpu.CompilerParams(vmem_limit_bytes=60 * MEBI),
        cost_estimate=pl.CostEstimate(
            flops=0, bytes_accessed=arrays[0].size // 8, transcendentals=0
        ),
        name="unpack_rows",
    )(place.reshape(1), *arrays)


def row_mean(blocks):
    return sum(jnp.sum(b, 1, keepdims=True) for b in blocks) / (len(blocks) * blocks[0].shape[1])


def normalize(blocks):
    center = row_mean(blocks)
    inverse = lax.rsqrt(row_mean([b * b for b in blocks]) - center * center + EPSILON)
    return [(b - center) * inverse for b in blocks], inverse


def norm_back(upstream, scaled, inverse, gains):
    grads = [u * g for u, g in zip(upstream, gains)]
    plain = row_mean(grads)
    cross = row_mean([g * x for g, x in zip(grads, scaled)])
    return [inverse * (g - plain - x * cross) for g, x in zip(grads, scaled)]


def cut(values, width):
    return [values[:, at : at + width] for at in range(0, values.shape[1], width)]


def add_rows(ref, values, at=0):
    ref[:, at : at + values.shape[1]] += jnp.sum(values, 0, keepdims=True)


def grid_of(refs, shape):
    outer, inner = shape
    return [refs[i * inner : (i + 1) * inner] for i in range(outer)]


def project_kernel(shape, gain_ref, shift_ref, bias_ref, *refs):
    rows, cols = shape
    x_refs, weights = refs[:rows], grid_of(refs[rows : rows + rows * cols], shape)
    normed_ref, packed_ref = refs[rows + rows * cols :]
    width, block = weights[0][0].shape
    gains, shifts = cut(gain_ref[...], width), cut(shift_ref[...], width)
    for some in PIECES:
        scaled, _ = normalize([x[some, :].astype(F32) for x in x_refs])
        normed = [(x * g + b).astype(BF) for x, g, b in zip(scaled, gains, shifts)]
        for i, n in enumerate(normed):
            normed_ref[some, i * width : (i + 1) * width] = n
        for j in range(cols):
            total = sum(dot_nn(n, weights[i][j][...]) for i, n in enumerate(normed))
            where = slice(j * block, (j + 1) * block)
            packed_ref[some, where] = (total + bias_ref[:, where]).astype(BF)


def swap_halves(values):
    return jnp.concatenate([values[:, HD:], values[:, :HD]], 1)


def attend_kernel(p_ref, o_ref):
    first, second, third = p_ref[:, :128], p_ref[:, 128:256], p_ref[:, 256:]
    low = lax.broadcasted_iota(jnp.int32, (1, 128), 1) < HD
    zero, one = jnp.zeros((), BF), jnp.ones((), BF)
    queries = (jnp.where(low, first, zero), jnp.where(low, swap_halves(second), zero))
    keys = (swap_halves(first), third)
    values = (jnp.where(low, second, one), jnp.where(low, one, third))
    scale = HD**-0.5 * LOG2E
    keep = lax.broadcasted_iota(jnp.int32, (1, PAD - KEYS_A), 1) < SEQ - KEYS_A
    units = [(slice(*cut), h) for cut in zip(QUERY_CUTS, QUERY_CUTS[1:]) for h in range(2)]
    scores = [
        (dot_nt(queries[h][some], keys[h][:KEYS_A]), dot_nt(queries[h][some], keys[h][KEYS_A:]))
        for some, h in units
    ]
    weights = []
    for sa, sb in scores:
        sb = jnp.where(keep, sb, -1e30)
        top = jnp.maximum(jnp.max(sa, 1, keepdims=True), jnp.max(sb, 1, keepdims=True)) * scale
        weights.append([jnp.exp2(v * scale - top).astype(BF) for v in (sa, sb)])
    outs = [
        dot_nn(pa, values[h][:KEYS_A]) + dot_nn(pb, values[h][KEYS_A:])
        for (_, h), (pa, pb) in zip(units, weights)
    ]
    for n in range(0, len(units), 2):
        mixed, totals = jnp.where(low, *outs[n : n + 2]), jnp.where(low, *outs[n : n + 2][::-1])
        o_ref[units[n][0], :] = (mixed / swap_halves(totals)).astype(BF)


def attend(packed, first, some, into, after):
    tokens, width = packed.shape
    pairs = width // (6 * HD)
    return call(
        attend_kernel,
        "attend",
        (some, tokens // PAD),
        [(pl.BlockSpec((PAD, 6 * HD), lambda h, i: (i, first + h)), packed)],
        [
            (
                pl.BlockSpec((PAD, 2 * HD), lambda h, i: (i, first + h)),
                (tokens, pairs * 2 * HD),
                BF,
            )
        ],
        tokens * PAD * some * 2 * HD * 5,
        after,
        into,
    )[0]


def attend_back_kernel(p_ref, g_ref, o_ref):
    first, second, third = p_ref[:, :128], p_ref[:, 128:256], p_ref[:, 256:]
    grad = g_ref[...]
    low = lax.broadcasted_iota(jnp.int32, (1, 128), 1) < HD
    zero = jnp.zeros((), BF)
    turned = [swap_halves(v) for v in (first, second, third)]
    queries = (jnp.where(low, first, zero), jnp.where(low, turned[1], zero))
    keys, values = (turned[0], third), (second, third)
    grads = (jnp.where(low, grad, zero), jnp.where(low, zero, grad))
    query_right = (turned[0], turned[1])
    key_right = (turned[0], turned[2])
    scale = HD**-0.5
    edge = PAD - 16
    keep = lax.broadcasted_iota(jnp.int32, (PAD - edge, 1), 0) < SEQ - edge
    units = [(slice(at, min(PAD, at + 256)), h) for at in range(0, PAD, 256) for h in range(2)]
    products = [
        (dot_nt(keys[h], queries[h][some]), dot_nt(values[h], grads[h][some])) for some, h in units
    ]
    lows = []
    for scores, weight_grad in products:
        sa, sb = scores[:edge], jnp.where(keep, scores[edge:], -1e30)
        top = jnp.maximum(jnp.max(sa, 0, keepdims=True), jnp.max(sb, 0, keepdims=True))
        top = top * (scale * LOG2E)
        weights = jnp.concatenate([jnp.exp2(s * (scale * LOG2E) - top) for s in (sa, sb)], 0)
        share = 1.0 / jnp.sum(weights, 0, keepdims=True)
        product = weights * weight_grad
        row_dot = jnp.sum(product, 0, keepdims=True) * share
        score_low = (product - weights * row_dot) * share
        lows.append(((weights * share).astype(BF), score_low.astype(BF)))
    value_grad, key_grad, query_grad = [0.0, 0.0], [0.0, 0.0], [[], []]
    for (some, h), (weights, score_low) in zip(units, lows):
        value_grad[h] += dot_nn(weights, grad[some])
        key_grad[h] += dot_nn(score_low, query_right[h][some])
        query_grad[h].append(dot_tn(key_right[h], score_low).T)
    query_grad = [jnp.concatenate(q, 0) for q in query_grad]
    o_ref[:, :128] = (jnp.where(low, query_grad[0], key_grad[0]) * scale).astype(BF)
    o_ref[:, 128:256] = jnp.where(low, value_grad[0], query_grad[1] * scale).astype(BF)
    o_ref[:, 256:] = jnp.where(low, key_grad[1] * scale, value_grad[1]).astype(BF)


def attend_back(packed, grad, cols, pair, slot, slots, into, after):
    tokens, width = packed.shape
    block = width // (6 * HD) // cols
    return call(
        attend_back_kernel,
        "attend_back",
        (cols, tokens // PAD),
        [
            (pl.BlockSpec((PAD, 6 * HD), lambda j, i: (i, j * block + pair)), packed),
            (pl.BlockSpec((PAD, 2 * HD), lambda j, i: (i, j * block + pair)), grad),
        ],
        [
            (
                pl.BlockSpec((PAD, 6 * HD), lambda j, i: (i, j * slots + slot)),
                (tokens, cols * slots * 6 * HD),
                BF,
            )
        ],
        tokens * PAD * cols * 2 * HD * 12,
        after,
        into,
        LIGHT,
    )[0]


def output_kernel(shape, bias_ref, gain_ref, shift_ref, mixed_ref, *refs):
    rows, cols = shape
    x_refs, weights = refs[:rows], grid_of(refs[rows : rows + rows * cols], shape)
    middle_ref, normed_ref = refs[rows + rows * cols :]
    block, width = weights[0][0].shape
    spans = [slice(i * width, (i + 1) * width) for i in range(rows)]
    totals = []
    for some in PIECES:
        mixed = cut(mixed_ref[some, :], block)
        totals.append(
            [
                sum(dot_nn(m, weights[i][j][...]) for j, m in enumerate(mixed))
                for i in range(rows)
            ]
        )
    for some, total in zip(PIECES, totals):
        middle = []
        for i, where in enumerate(spans):
            middle.append(x_refs[i][some, :].astype(F32) + total[i] + bias_ref[:, where])
            middle_ref[some, where] = middle[-1]
        scaled, _ = normalize(middle)
        for x, where in zip(scaled, spans):
            normed = x * gain_ref[:, where] + shift_ref[:, where]
            normed_ref[some, where] = normed.astype(BF)


def expand_kernel(shape, bias_ref, normed_ref, *refs):
    rows, cols = shape
    weights = grid_of(refs[: rows * cols], shape)
    hidden_ref, slope_ref = refs[rows * cols :]
    depth, block = weights[0][0].shape
    cuts = [
        (some, j, at)
        for some in PIECES
        for j in range(cols)
        for at in range(0, block, min(block, EXPAND_CUT))
    ]
    normed = {some.start: cut(normed_ref[some, :], depth) for some in PIECES}
    wide = min(block, EXPAND_CUT)
    totals = [
        sum(
            dot_nn(n, weights[i][j][:, at : at + wide])
            for i, n in enumerate(normed[some.start])
        )
        for some, j, at in cuts
    ]
    for (some, j, at), total in zip(cuts, totals):
        where = slice(j * block + at, j * block + at + wide)
        before = total + bias_ref[:, where]
        below = 0.5 + 0.5 * lax.erf(before * ROOT_HALF)
        hidden_ref[some, where] = (before * below).astype(BF)
        density = jnp.exp2(before * before * (-0.5 * LOG2E)) * DENSITY
        slope_ref[some, where] = (below + before * density).astype(BF)


def reduce_kernel(shape, valid_ref, bias_ref, hidden_ref, middle_ref, *refs):
    rows, cols = shape
    weights, o_refs = grid_of(refs[: rows * cols], shape), refs[rows * cols :]
    block, width = weights[0][0].shape
    valid = valid_ref[pl.program_id(0)].astype(F32)
    for i in range(rows):
        total = sum(
            dot_nn(hidden_ref[:, j * block : (j + 1) * block], weights[i][j][...])
            for j in range(cols)
        )
        where = slice(i * width, (i + 1) * width)
        o_refs[i][...] = ((middle_ref[:, where] + total + bias_ref[:, where]) * valid).astype(BF)


def reduce_back_kernel(shape, slope_ref, *refs):
    rows, cols = shape
    g_refs, weights = refs[:rows], grid_of(refs[rows : rows + rows * cols], shape)
    before_ref, reduce_bias_ref, expand_bias_ref = refs[rows + rows * cols :]

    @pl.when(pl.program_id(0) == 0)
    def _():
        reduce_bias_ref[...] = jnp.zeros_like(reduce_bias_ref)
        expand_bias_ref[...] = jnp.zeros_like(expand_bias_ref)

    block, width = weights[0][0].shape
    lows = [g[...] for g in g_refs]
    for i, low in enumerate(lows):
        add_rows(reduce_bias_ref, low.astype(F32), i * width)
    for j in range(cols):
        total = sum(dot_nt(low, weights[i][j][...]) for i, low in enumerate(lows))
        where = slice(j * block, (j + 1) * block)
        total = total * slope_ref[:, where].astype(F32)
        add_rows(expand_bias_ref, total, j * block)
        before_ref[:, where] = total.astype(BF)


def expand_back_kernel(shape, gain_ref, before_ref, middle_ref, *refs):
    rows, cols = shape
    g_refs, refs = refs[:rows], refs[rows:]
    count = rows * cols
    expand, output = grid_of(refs[:count], shape), grid_of(refs[count : 2 * count], shape)
    refs = refs[2 * count :]
    middle_grad_ref, mixed_low_ref, gain_grad, shift_grad, bias_grad = refs[:5]
    low_refs = refs[5:]

    @pl.when(pl.program_id(0) == 0)
    def _():
        for ref in (gain_grad, shift_grad, bias_grad):
            ref[...] = jnp.zeros_like(ref)

    width, block = expand[0][0].shape
    spans = [slice(i * width, (i + 1) * width) for i in range(rows)]
    heads = output[0][0].shape[0]
    upstreams = [
        [
            sum(
                dot_nt(before_ref[some, j * block : (j + 1) * block], expand[i][j][...])
                for j in range(cols)
            )
            for i in range(rows)
        ]
        for some in PIECES
    ]
    for some, upstream in zip(PIECES, upstreams):
        scaled, inverse = normalize(cut(middle_ref[some, :], width))
        parts = norm_back(upstream, scaled, inverse, cut(gain_ref[...], width))
        lows = []
        for i, part in enumerate(parts):
            add_rows(gain_grad, upstream[i] * scaled[i], i * width)
            add_rows(shift_grad, upstream[i], i * width)
            grad = g_refs[i][some, :].astype(F32) + part
            add_rows(bias_grad, grad, i * width)
            middle_grad_ref[some, spans[i]] = grad
            lows.append(grad.astype(BF))
            low_refs[i][some, :] = lows[-1]
        for j in range(cols):
            total = sum(dot_nt(low, output[i][j][...]) for i, low in enumerate(lows))
            mixed_low_ref[some, j * heads : (j + 1) * heads] = total.astype(BF)


def project_back_kernel(shape, parts, gain_ref, middle_ref, *refs):
    rows, cols = shape
    packed, refs = refs[:parts], refs[parts:]
    x_refs, weights = refs[:rows], grid_of(refs[rows : rows + rows * cols], shape)
    refs = refs[rows + rows * cols :]
    o_refs, (gain_grad, shift_grad), bias_grads = refs[:rows], refs[rows : rows + 2], refs[rows + 2 :]

    @pl.when(pl.program_id(0) == 0)
    def _():
        for ref in refs[rows:]:
            ref[...] = jnp.zeros_like(ref)

    width = weights[0][0].shape[0]
    for p in range(parts):
        add_rows(bias_grads[p], packed[p][...].astype(F32))
    upstreams = []
    for piece in PIECES:
        upstream = [0.0] * rows
        at = 0
        for p in range(parts):
            some = packed[p].shape[1] // cols
            for j in range(cols):
                grad = packed[p][piece, j * some : (j + 1) * some]
                for i in range(rows):
                    upstream[i] += dot_nt(grad, weights[i][j][:, at : at + some])
            at += some
        upstreams.append(upstream)
    for piece, upstream in zip(PIECES, upstreams):
        scaled, inverse = normalize([x[piece, :].astype(F32) for x in x_refs])
        grads = norm_back(upstream, scaled, inverse, cut(gain_ref[...], width))
        for i, grad in enumerate(grads):
            add_rows(gain_grad, upstream[i] * scaled[i], i * width)
            add_rows(shift_grad, upstream[i], i * width)
            total = middle_ref[piece, i * width : (i + 1) * width] + grad
            o_refs[i][piece, :] = total.astype(o_refs[i].dtype)


def outer_kernel(rights, received, whole_width, a_ref, *refs):
    b_refs, refs = refs[:rights], refs[rights:]
    received, o_refs = refs[:received], refs[received:]
    height, width = o_refs[0].shape
    left = a_ref[...]
    at = 0
    for b_ref in b_refs:
        total = dot_tn(left, b_ref[...])
        where = slice(at, at + total.shape[1])
        for ref in received:
            total += ref[:, where].astype(F32)
        total = total.astype(BF)
        if width < whole_width:
            o_refs[at // width][...] = total
        else:
            for n, o_ref in enumerate(o_refs):
                o_ref[:, where] = total[n * height : (n + 1) * height]
        at = where.stop


def outer(left, rights, left_part, right_part, name, after, received=(), splits=(1, 1)):
    tokens = left.shape[0]
    (li, lw), (ri, rw) = left_part, right_part
    bl, br = min(lw, 1024), 1024 if rw % 1024 == 0 else rw
    down, across = splits
    tile = pl.BlockSpec((bl, br), lambda i, j: (i, j))
    part = pl.BlockSpec((bl // down, br // across), lambda i, j: (i, j))
    spec = pl.BlockSpec((tokens, br // len(rights)), lambda i, j: (0, ri * (rw // br) + j))
    return call(
        partial(outer_kernel, len(rights), len(received), br),
        name,
        (lw // bl, rw // br),
        [(pl.BlockSpec((tokens, bl), lambda i, j: (0, li * (lw // bl) + i)), left)]
        + [(spec, right) for right in rights]
        + [(tile, r) for r in received],
        [(part, (lw // down, rw // across), BF)] * (down * across),
        tokens * lw * rw,
        after,
        weight=1 if name in ("reduce_outer", "expand_outer") else LIGHT,
    )


def body(
    block_input,
    image_valid,
    first_gain,
    first_shift,
    attend_weight,
    attend_bias,
    output_weight,
    output_bias,
    second_gain,
    second_shift,
    expand_weight,
    expand_bias,
    reduce_weight,
    reduce_bias,
    output_grad,
):
    rows, cols = lax.axis_size("row"), lax.axis_size("col")
    row_index, col_index = lax.axis_index("row"), lax.axis_index("col")
    local_rows, width = block_input.shape
    local_images = local_rows // SEQ
    images = local_images // rows
    tokens = images * PAD
    hidden_width = expand_weight.shape[1] * cols
    shape = (rows, cols)
    step = (images,)

    local_valid = lax.dynamic_slice_in_dim(image_valid, col_index * local_images, local_images)

    def to_tokens(values, masked, after=()):
        parts = pack_rows(values, row_index, local_valid, masked, after)
        return [shift(part, "row", -s) if s else part for s, part in enumerate(parts)]

    def sent(parts):
        return [shift(a, "row", s) if s else a for s, a in enumerate(parts)]

    features = jnp.stack(
        [first_gain, first_shift, output_bias, second_gain, second_shift, reduce_bias]
    )
    features = jnp.concatenate(gather_blocks(features, "row"), 1).astype(F32)
    first_gain, first_shift, output_bias, second_gain, second_shift, reduce_bias = jnp.split(
        features, 6, 0
    )
    biases = jnp.stack(gather_blocks(jnp.concatenate([attend_bias, expand_bias]), "col"))
    biases = biases.astype(F32)
    pairs = biases[:, : attend_bias.shape[0]].reshape(-1, 2, HD)
    attend_bias = jnp.stack([pairs[:, 0], jnp.zeros_like(pairs[:, 0]), pairs[:, 1]], 1)
    attend_bias = attend_bias.reshape(1, 3 * D)
    expand_bias = biases[:, -expand_bias.shape[0] :].reshape(1, -1)
    valid = lax.dynamic_slice_in_dim(
        image_valid, col_index * local_images + row_index * images, images
    )

    inputs = to_tokens(block_input, False)
    attend_shares, expand_shares = hold(fetch_shares([attend_weight, expand_weight]), inputs[0])
    attend_blocks = gather_shares(attend_weight, attend_shares)
    output_rows = gather_blocks(hold(output_weight, inputs), "row")

    def flat(blocks):
        return [(whole(b), b) for some in blocks for b in some]

    def row_blocks(arrays):
        return [(by_image(width), a) for a in arrays]

    def full(array):
        return (whole(array), array)

    def image(array):
        return (by_image(array.shape[1]), array)

    def out(columns, dtype):
        return (by_image(columns), (tokens, columns), dtype)

    def total(columns):
        return (pl.BlockSpec((1, columns), lambda i: (0, 0)), (1, columns), F32)

    scalars = (pl.BlockSpec(memory_space=pltpu.SMEM), valid)

    first_normed, packed = call(
        partial(project_kernel, shape),
        "project",
        step,
        [full(first_gain), full(first_shift), full(attend_bias)]
        + row_blocks(inputs)
        + flat(attend_blocks),
        [out(D, BF), out(3 * D, BF)],
        tokens * 3 * D * D,
    )
    grads = to_tokens(output_grad, True, (packed,))
    (reduce_shares,) = fetch_shares([hold(reduce_weight, packed)])
    pairs = packed.shape[1] // (6 * HD)
    mixed = attend(packed, 0, pairs // 4, None, (*expand_shares, *reduce_shares, grads[0]))
    expand_blocks = gather_shares(expand_weight, expand_shares, mixed)
    reduce_shares = hold(reduce_shares, mixed)
    mixed = attend(packed, pairs // 4, pairs - pairs // 4, mixed, reduce_shares)
    output_blocks = [gather_blocks(block, "col") for block in hold(output_rows, mixed)]
    middle, second_normed = call(
        partial(output_kernel, shape),
        "output",
        step,
        [full(output_bias), full(second_gain), full(second_shift), image(mixed)]
        + row_blocks(inputs)
        + flat(output_blocks),
        [out(D, F32), out(D, BF)],
        tokens * D * D,
    )
    reduce_blocks = gather_shares(reduce_weight, reduce_shares, second_normed)
    hidden, slope = call(
        partial(expand_kernel, shape),
        "expand",
        step,
        [full(expand_bias), image(second_normed)] + flat(expand_blocks),
        [out(hidden_width, BF), out(hidden_width, BF)],
        tokens * D * hidden_width,
        (*reduce_blocks[0][1:], *reduce_blocks[-1][:1]),
    )
    def add_parts(parts, axis, after=None):
        held = parts[0].astype(F32)
        others = [shift(part, axis, s) for s, part in enumerate(parts) if s]
        for other in others if after is None else hold(others, after):
            held = held + other.astype(F32)
        return held

    def places(left, rights, over_left, j):
        lw, rw = left.shape[1], sum(r.shape[1] for r in rights)
        return ((j, lw // cols), (0, rw)) if over_left else ((0, lw), (j, rw // cols))

    def outer_others(left, rights, over_left, name, after=()):
        received = []
        for j in range(1, cols):
            (block,) = outer(left, rights, *places(left, rights, over_left, j), name, after)
            received.append(shift(block, "col", j))
            after = (block,)
        return received, after

    def outer_own(left, rights, over_left, name, others, after=()):
        received, order = others
        splits = (1, rows) if over_left else (rows, 1)
        where = places(left, rights, over_left, 0)
        return outer(left, rights, *where, name, (*order, *after), received, splits)

    def share_of(held, after=None):
        received = [shift(part, "row", s) for s, part in enumerate(held) if s]
        total = held[0].astype(F32)
        for part in received if after is None else hold(received, after):
            total = total + part.astype(F32)
        return total.astype(BF), received

    reduce_others = outer_others(hidden, grads, True, "reduce_outer", reduce_blocks[-1][:1])
    before_low, reduce_bias_grad, expand_bias_grad = call(
        partial(reduce_back_kernel, shape),
        "reduce_back",
        step,
        [image(slope)] + row_blocks(grads) + flat(reduce_blocks),
        [out(hidden_width, BF), total(D), total(hidden_width)],
        tokens * D * hidden_width,
        reduce_others[1],
        weight=LIGHT,
    )
    reduce_held = outer_own(hidden, grads, True, "reduce_outer", reduce_others, (before_low,))
    reduce_share, reduce_received = share_of(reduce_held)
    expand_others = outer_others(
        second_normed, [before_low], False, "expand_outer", reduce_held[:1]
    )
    middle_grad, mixed_low, second_gain_grad, second_shift_grad, output_bias_grad, *middle_lows = call(
        partial(expand_back_kernel, shape),
        "expand_back",
        step,
        [full(second_gain), image(before_low), image(middle)]
        + row_blocks(grads)
        + flat(expand_blocks)
        + flat(output_blocks),
        [out(D, F32), out(D, BF), total(D), total(D), total(D)] + [out(width, BF)] * rows,
        tokens * D * (hidden_width + D),
        expand_others[1],
        weight=LIGHT,
    )
    expand_held = outer_own(
        second_normed, [before_low], False, "expand_outer", expand_others, (middle_grad, *reduce_received)
    )
    output_others = outer_others(mixed, middle_lows, True, "output_outer", expand_held[:1])
    output_held = outer_own(mixed, middle_lows, True, "output_outer", output_others)

    reduce_weight_grad = lax.psum(reduce_share, "dp")
    expand_share, expand_received = share_of(expand_held)
    output_share, _ = share_of(output_held)
    expand_weight_grad = lax.psum(hold(expand_share, reduce_weight_grad), "dp")
    pairs = 3 * D // (6 * HD) // cols
    counts = [pairs - 2, 1, 1] if pairs > 2 else [pairs]
    packed_lows, held, shares, arrived, pair = [], [], [], (), 0
    ready = output_held[:1]
    for g, count in enumerate(counts):
        packed_low = None
        for slot in range(count):
            packed_low = attend_back(
                packed, mixed_low, cols, pair, slot, count, packed_low, ready
            )
            ready = []
            if pair == 0:
                results = call(
                    partial(reduce_kernel, shape),
                    "reduce",
                    step,
                    [scalars, full(reduce_bias), image(hidden), image(middle)] + flat(reduce_blocks),
                    [out(width, BF)] * rows,
                    tokens * D * hidden_width,
                    (packed_low,),
                    weight=LIGHT,
                )
                block_output = unpack_rows([[part] for part in sent(results)], row_index, BF)
                ready = [results[0], *expand_received]
            pair += 1
        packed_lows.append(packed_low)
        last = (reduce_weight_grad,) if g == 0 else (block_output,)
        if g == 2:
            last = (expand_weight_grad, output_share, *shares)
        others = outer_others(first_normed, [packed_low], False, "project_outer", last)
        held.append(outer_own(first_normed, [packed_low], False, "project_outer", others))
        ready = (held[g][0],)
        if g < 2:
            shares.append(share_of(held[g])[0])
    output_weight_grad, first_sum = lax.psum(
        hold((output_share, shares[0]), expand_weight_grad), "dp"
    )

    halves = 2 if images % 2 == 0 else 1
    some = images // halves
    input_grads, sums = [], 0.0
    for half in range(halves):

        def later(array):
            place = half * some
            spec = pl.BlockSpec((PAD, array.shape[1]), lambda i: (i + place, 0))
            return (spec, array)

        def here(dtype):
            return (by_image(width), (some * PAD, width), dtype)

        results = call(
            partial(project_back_kernel, shape, len(counts)),
            "project_back",
            (some,),
            [full(first_gain), later(middle_grad)]
            + [later(p) for p in packed_lows]
            + [later(x) for x in inputs]
            + flat(attend_blocks),
            [here(F32)]
            + [here(BF)] * (rows - 1)
            + [total(D), total(D)]
            + [total(p.shape[1]) for p in packed_lows],
            some * PAD * 3 * D * D,
            ready,
            weight=LIGHT,
        )
        input_grads.append(sent(results[:rows]))
        if half == 0 and len(counts) > 1:
            share, arrived = share_of(held[-1], results[0])
            shares.append(share)
        ready = (results[0], *arrived)
        packed_sums = [v.reshape(cols, -1, 3, HD) for v in results[rows + 2 :]]
        late = (*results[rows : rows + 2], jnp.concatenate(packed_sums, 1))
        sums = late if half == 0 else jax.tree.map(jnp.add, sums, late)
    input_grad = unpack_rows(list(zip(*input_grads)), row_index, F32)
    first_gain_grad, first_shift_grad, packed_sums = sums
    attend_weight_grad = [first_sum]
    if len(shares) > 1:
        attend_weight_grad.append(sum_shares(jnp.concatenate(shares[1:], 1), "dp"))
    attend_weight_grad = jnp.concatenate(attend_weight_grad, 1)

    feature_grads = jnp.concatenate(
        [
            first_gain_grad,
            first_shift_grad,
            output_bias_grad,
            second_gain_grad,
            second_shift_grad,
            reduce_bias_grad,
        ]
    )
    attend_bias_grad = jnp.stack([packed_sums[:, :, 0], packed_sums[:, :, 2]], 2)
    attend_bias_grad = attend_bias_grad.reshape(cols, -1)
    bias_grads = jnp.concatenate([attend_bias_grad, expand_bias_grad.reshape(cols, -1)], 1)
    bias_grads = add_parts(list(bias_grads), "col")
    feature_grads = sum_all(feature_grads.reshape(-1), "col")
    small = hold(jnp.concatenate([feature_grads, bias_grads]), input_grads[0][-1])
    small = hold(sum_all(small, "dp"), input_grads[-1][-1])
    feature_grads, bias_grads = small[: 6 * D].reshape(6, D), small[6 * D :]
    feature_grads = add_parts(jnp.split(feature_grads, rows, 1), "row")
    bias_grads = sum_all(bias_grads, "row")
    split = attend_bias_grad.shape[1]
    return (
        block_output,
        input_grad,
        feature_grads[0],
        feature_grads[1],
        attend_weight_grad.astype(F32),
        bias_grads[:split],
        output_weight_grad.astype(F32),
        feature_grads[2],
        feature_grads[3],
        feature_grads[4],
        expand_weight_grad.astype(F32),
        bias_grads[split:],
        reduce_weight_grad.astype(F32),
        feature_grads[5],
    )


def solution(mesh):
    tokens = P(("dp", "col"), "row")
    by_row, by_col = P("row"), P("col")
    up, down = P("row", "col"), P("col", "row")
    params = (by_row, by_row, up, by_col, down, by_row, by_row, by_row, up, by_col, down, by_row)
    return jax.shard_map(
        body,
        mesh=mesh,
        in_specs=(tokens, P("dp")) + params + (tokens,),
        out_specs=(tokens, tokens) + params,
        check_vma=False,
    )
```
